128 devices in a mesh: tm: 16 (over x_lo, y, core), tensor: 2 (over x_hi), section: 4 (over z).
Axes of the slice: x: 4 (x_hi: 2, x_lo: 2; x = x_hi * 2 + x_lo), y: 4, z: 4, core: 2. Of those that a mesh axis runs over, the one named last changes fastest.
Arguments:
- frames: bfloat16 [32768, 1280], P(('tm', 'section')), may hold values from -6 to 6
- returned: bfloat16 [32768, 1280], P('tm', 'section'), may hold values from -6 to 6
- norm_gain: float32 [1280], replicated, may hold values from 0.5 to 1.5
- weight_in: bfloat16 [2, 1280, 1280], P(None, None, 'tensor'), may hold values from -0.15625 to 0.15625
- kernel: float32 [31, 1280], P(None, 'tensor'), may hold values from -1.5 to 1.5
- weight_out: bfloat16 [1280, 1280], P('tensor'), may hold values from -0.15625 to 0.15625
- block_utt: int32 [256], replicated, may hold values from 0 to 63, as said below
- block_fill: int32 [256], replicated, may hold values from 1 to 128, as said below
Outputs:
- grad_frames: bfloat16 [32768, 1280], P(('tm', 'section'))
- grad_in: float32 [2, 1280, 1280], P(None, ('tm', 'section'), 'tensor')
- grad_out: float32 [1280, 1280], P('tensor', ('tm', 'section'))
- grad_kernel: float32 [31, 1280], P(None, 'tensor')
- grad_gain: float32 [1280], replicated
The draws below stay inside these ranges and needn't reach their ends.
Inputs may be any that keep to these rules, and one draw needn't show every extreme that they name: `block_utt`: there are exactly 64 utterances. Utterance numbers start at 0 in the first block, never fall, and rise by at most one from a block to the next; every utterance begins at a block's first frame. `block_fill`: every block holds 128 valid frames except the last block of an utterance, whose valid frames come first and the rest is padding.
All inputs are finite; a program needn't handle non-finite values.
Results may differ from the reference program's by a relative error of at most 0.0065.
Values may be sent and summed in bfloat16 or wider, within the bound.
No kernel may reach another device: no remote copies, remote signals or barrier semaphores. Data moves between devices by JAX's collectives and lax.ppermute only.
A program may use at most 128 MiB of HBM per device.

```python
import jax
import jax.numpy as jnp
from jax import lax

D = 1280
KW = 31
BLOCK = 128
TOKENS = 32768
NBLK = 256


def utterance_layout(key):
    order = jax.random.permutation(key, NBLK - 1) + 1
    chosen = order[:NBLK // 4 - 1]
    starts = jnp.zeros((NBLK,), dtype=bool).at[0].set(True).at[chosen].set(True)
    numbers = jnp.cumsum(starts.astype(jnp.int32)) - 1
    closing = jnp.concatenate([starts[1:], jnp.array([True])])
    tails = jax.random.randint(jax.random.fold_in(key, 11), (NBLK,), 1, BLOCK + 1)
    fills = jnp.where(closing, tails, BLOCK).at[NBLK - 1].set(1)
    return (numbers.astype(jnp.int32), fills.astype(jnp.int32))


def draw_block_utt(key, part):
    return utterance_layout(key)[0]


def draw_block_fill(key, part):
    return utterance_layout(key)[1]


def with_spikes(drawn, own_key, source, target, parts, factor):
    def block_of(axis_at):
        return (jnp.arange(drawn.shape[axis_at]) // (drawn.shape[axis_at] // parts)).reshape((-1,) + (1,) * (drawn.ndim - 1 - axis_at))

    first = jax.random.permutation(own_key, parts)[block_of(target)]
    other_side = (block_of(target) + parts // 2) % parts
    return jnp.where((block_of(source) == first) | (block_of(source) == other_side), factor * drawn, drawn)


def steps_of(own_key, extent, cuts, smallest, high):
    factor_of, own = 1.0, jax.random.fold_in(own_key, 6)
    for dim, blocks in cuts:
        steps = jnp.exp(jax.random.uniform(jax.random.fold_in(own, dim), (blocks,), jnp.float32, smallest / len(cuts), high / len(cuts)))
        factor_of = factor_of * jnp.repeat(steps, extent[dim] // blocks).reshape([-1 if axis == dim else 1 for axis in range(len(extent))])
    return factor_of


def scatter_about(stream_key, extent, deviation, reach, cuts=(), kind=jnp.bfloat16):
    values = deviation * jax.random.normal(stream_key, extent, jnp.float32)
    if cuts:
        values = values * steps_of(stream_key, extent, cuts, -0.22, 0.18)
    return jnp.clip(values, -reach, reach).astype(kind)


def gaussian_with(key, dims, width, limit, pieces, heavy, kind=jnp.bfloat16):
    values = width * jax.random.normal(key, dims, jnp.float32)
    if pieces:
        values = values * steps_of(key, dims, pieces, -0.22, 0.18)
    return jnp.clip(with_spikes(values, jax.random.fold_in(key, 3), *heavy), -limit, limit).astype(kind)


def setup_inputs(seed: int = 0) -> dict:
    seeds = jax.random.split(jax.random.key(seed), 9)
    return {
        "frames": scatter_about(seeds[0], (TOKENS, D), 1.0, 6.0, ((0, 64),)),
        "returned": gaussian_with(seeds[1], (TOKENS, D), 1.0, 6.0, ((0, 16), (1, 4)), (0, 1, 16, 2.0)),
        "norm_gain": jnp.clip(1.0 + 0.1 * jax.random.normal(seeds[2], (D,), jnp.float32), 0.5, 1.5),
        "weight_in": scatter_about(seeds[3], (2, D, D), D ** -0.5, 0.15625, ((2, 2),)),
        "kernel": scatter_about(seeds[4], (KW, D), 0.25, 1.5, ((1, 2),), jnp.float32),
        "weight_out": scatter_about(seeds[5], (D, D), D ** -0.5, 0.15625, ((0, 2),)),
        "block_utt": draw_block_utt(jax.random.fold_in(seeds[8], 71), 0),
        "block_fill": draw_block_fill(jax.random.fold_in(seeds[8], 71), 0),
    }


epsilon = 1e-05

def frame_tables(block_utt, block_fill):
    frame_pos = jnp.arange(TOKENS, dtype=jnp.int32)
    frame_utt = jnp.repeat(block_utt, BLOCK, total_repeat_length=TOKENS).astype(jnp.int32)
    frame_fill = jnp.repeat(block_fill, BLOCK, total_repeat_length=TOKENS).astype(jnp.int32)
    return (frame_utt, frame_pos % BLOCK < frame_fill)

def reference(frames, returned, norm_gain, weight_in, kernel, weight_out, block_utt, block_fill):
    frame_utt, valid_frame = frame_tables(block_utt, block_fill)
    valid_col = valid_frame.astype(jnp.float32)[:, None]
    half_taps = KW // 2
    as_float = frames.astype(jnp.float32)
    center = as_float - lax.optimization_barrier(jnp.mean(as_float, axis=1, keepdims=True))
    inv_scale = lax.rsqrt(lax.optimization_barrier(jnp.mean(center * center, axis=1, keepdims=True)) + epsilon)
    unit_frames = center * inv_scale
    normed = (unit_frames * norm_gain).astype(jnp.bfloat16)
    value_proj = jnp.dot(normed, weight_in[0], preferred_element_type=jnp.float32)
    gate_proj = jnp.dot(normed, weight_in[1], preferred_element_type=jnp.float32)
    gate_sigmoid = jax.nn.sigmoid(gate_proj)
    gated_units = (valid_col * value_proj * gate_sigmoid).astype(jnp.bfloat16)
    units_pad = jnp.pad(gated_units.astype(jnp.float32), ((half_taps, half_taps), (0, 0)))
    utt_pad = jnp.pad(frame_utt, (half_taps, half_taps), constant_values=-1)
    conv_out = jnp.zeros(gated_units.shape, jnp.float32)
    for offset in range(KW):
        same_utt = (utt_pad[offset:offset + TOKENS] == frame_utt)[:, None]
        conv_out = conv_out + kernel[offset] * jnp.where(same_utt, units_pad[offset:offset + TOKENS], 0.0)
    conv_sigmoid = jax.nn.sigmoid(conv_out)
    activated = (conv_out * conv_sigmoid).astype(jnp.bfloat16)
    grad_rows = jnp.where(valid_frame[:, None], returned, jnp.zeros_like(returned))
    grad_out = jnp.dot(activated.T, grad_rows, preferred_element_type=jnp.float32)
    grad_activated = jnp.dot(grad_rows, weight_out.T, preferred_element_type=jnp.float32)
    grad_conv = grad_activated * (conv_sigmoid + conv_out * conv_sigmoid * (1.0 - conv_sigmoid))
    conv_pad = jnp.pad(grad_conv, ((half_taps, half_taps), (0, 0)))
    kernel_rows = []
    grad_units = jnp.zeros(grad_conv.shape, jnp.float32)
    for offset in range(KW):
        same_utt = (utt_pad[offset:offset + TOKENS] == frame_utt)[:, None]
        kernel_rows.append(lax.optimization_barrier(jnp.sum(jnp.where(same_utt, units_pad[offset:offset + TOKENS], 0.0) * grad_conv, axis=0)))
        back_offset = 2 * half_taps - offset
        back_same = (utt_pad[back_offset:back_offset + TOKENS] == frame_utt)[:, None]
        grad_units = grad_units + kernel[offset] * jnp.where(back_same, conv_pad[back_offset:back_offset + TOKENS], 0.0)
    grad_kernel = jnp.stack(kernel_rows)
    grad_units = grad_units * valid_col
    grad_value = (grad_units * gate_sigmoid).astype(jnp.bfloat16)
    grad_gate = (grad_units * value_proj * gate_sigmoid * (1.0 - gate_sigmoid)).astype(jnp.bfloat16)
    grad_in = jnp.stack([jnp.dot(normed.T, grad_value, preferred_element_type=jnp.float32), jnp.dot(normed.T, grad_gate, preferred_element_type=jnp.float32)])
    grad_normed = jnp.dot(grad_value, weight_in[0].T, preferred_element_type=jnp.float32) + jnp.dot(grad_gate, weight_in[1].T, preferred_element_type=jnp.float32)
    grad_gain = lax.optimization_barrier(jnp.sum(grad_normed * unit_frames, axis=0))
    scaled_grad = grad_normed * norm_gain
    norm_back = inv_scale * (scaled_grad - lax.optimization_barrier(jnp.mean(scaled_grad, axis=1, keepdims=True)) - unit_frames * lax.optimization_barrier(jnp.mean(scaled_grad * unit_frames, axis=1, keepdims=True)))
    grad_frames = (returned.astype(jnp.float32) + norm_back).astype(jnp.bfloat16)
    return (grad_frames, grad_in, grad_out, grad_kernel, grad_gain)
```

```python
import jax
import jax.numpy as jnp
import numpy as np
from jax import lax
from jax.sharding import Mesh
from jax.sharding import PartitionSpec as P

BLOCK = 128
EPSILON = 1e-05
BF16 = jnp.bfloat16
F32 = jnp.float32

FRAMES = ("xl", "y", "core", "section")
CHIPS = ("xl", "y", "section")
EVERY = ("xl", "y", "core", "tensor", "section")


def swap(value, axis):
    return lax.ppermute(value, axis, [(0, 1), (1, 0)])


def extended(shard, width):
    peers, length = (lax.axis_size(FRAMES), shard.shape[0])
    up = [(i, (i + 1) % peers) for i in range(peers - 1)]
    down = [(j, i) for i, j in up]
    before = lax.ppermute(shard[length - width :], FRAMES, up)
    after = lax.ppermute(shard[:width], FRAMES, down)
    return jnp.concatenate([before, shard, after], axis=0)


def core_rows(array, core):
    parts = array.reshape(8, 2, 80, array.shape[1])
    return lax.dynamic_index_in_dim(parts, core, 1, keepdims=False).reshape(640, array.shape[1])


def body(frames, returned, norm_gain, weight_in, kernel, weight_out, block_utt, block_fill):
    frame_count = frames.shape[0]
    tap_count = kernel.shape[0]
    half_taps = tap_count // 2
    core = lax.axis_index("core")
    first_block = lax.axis_index(FRAMES) * (frame_count // BLOCK)
    blocks = frame_count // BLOCK
    arrived = lax.all_to_all(returned, "section", split_axis=0, concat_axis=1, tiled=True)

    padded_utt = jnp.concatenate([jnp.full((1,), -1, jnp.int32), block_utt, jnp.full((1,), -1, jnp.int32)])
    near_utt = lax.dynamic_slice(padded_utt, (first_block,), (blocks + 2,))
    fill = lax.dynamic_slice(block_fill, (first_block,), (blocks,))
    frame_utt = jnp.broadcast_to(near_utt[1:-1, None], (blocks, BLOCK)).reshape(-1)
    ext_utt = jnp.concatenate(
        [
            jnp.broadcast_to(near_utt[:1], (half_taps,)),
            frame_utt,
            jnp.broadcast_to(near_utt[-1:], (half_taps,)),
        ]
    )
    valid_frame = (jnp.arange(BLOCK, dtype=jnp.int32)[None, :] < fill[:, None]).reshape(-1)
    valid_col = valid_frame.astype(F32)[:, None]

    as_float = frames.astype(F32)
    center = as_float - jnp.mean(as_float, axis=1, keepdims=True)
    inv_scale = lax.rsqrt(jnp.mean(center * center, axis=1, keepdims=True) + EPSILON)
    unit_frames = center * inv_scale
    normed = (unit_frames * norm_gain).astype(BF16)
    value_proj = jnp.dot(normed, weight_in[0], preferred_element_type=F32)
    gate_proj = jnp.dot(normed, weight_in[1], preferred_element_type=F32)
    gate_sigmoid = jax.nn.sigmoid(gate_proj)
    gated_units = (valid_col * value_proj * gate_sigmoid).astype(BF16)
    units_ext = extended(gated_units, half_taps).astype(F32)
    conv_out = jnp.zeros(gated_units.shape, F32)
    for offset in range(tap_count):
        same_utt = (ext_utt[offset : offset + frame_count] == frame_utt)[:, None]
        conv_out = conv_out + kernel[offset] * jnp.where(
            same_utt, units_ext[offset : offset + frame_count], 0.0
        )
    conv_sigmoid = jax.nn.sigmoid(conv_out)
    activated = (conv_out * conv_sigmoid).astype(BF16)

    grad_rows = jnp.where(valid_frame[:, None], arrived, jnp.zeros_like(arrived))
    grad_activated = jnp.dot(grad_rows, weight_out.T, preferred_element_type=F32)
    grad_conv = grad_activated * (conv_sigmoid + conv_out * conv_sigmoid * (1.0 - conv_sigmoid))
    conv_ext = extended(grad_conv, half_taps)
    kernel_rows = []
    grad_units = jnp.zeros(grad_conv.shape, F32)
    for offset in range(tap_count):
        same_utt = (ext_utt[offset : offset + frame_count] == frame_utt)[:, None]
        kernel_rows.append(
            jnp.sum(
                jnp.where(same_utt, units_ext[offset : offset + frame_count], 0.0) * grad_conv,
                axis=0,
            )
        )
        back_offset = 2 * half_taps - offset
        back_same = (ext_utt[back_offset : back_offset + frame_count] == frame_utt)[:, None]
        grad_units = grad_units + kernel[offset] * jnp.where(
            back_same, conv_ext[back_offset : back_offset + frame_count], 0.0
        )
    kernel_part = jnp.stack(kernel_rows)
    grad_units = grad_units * valid_col
    grad_value = (grad_units * gate_sigmoid).astype(BF16)
    grad_gate = (grad_units * value_proj * gate_sigmoid * (1.0 - gate_sigmoid)).astype(BF16)

    normed_part = jnp.dot(grad_value, weight_in[0].T, preferred_element_type=F32) + jnp.dot(
        grad_gate, weight_in[1].T, preferred_element_type=F32
    )
    sent = normed_part.astype(BF16)
    other = swap(sent, "tensor")
    gain_part = jnp.sum(normed_part * unit_frames, axis=0)

    normed_t, rows_t = normed.T, grad_rows.T
    early = jnp.stack([core_rows(normed_t, 1 - core), core_rows(rows_t, 1 - core)])
    early_peer = swap(early, "core")
    activated_peer = swap(activated, "core")
    late = jnp.concatenate([grad_value, grad_gate], axis=1)
    late_peer = swap(late, "core")
    in_part = jnp.dot(core_rows(normed_t, core), late, preferred_element_type=F32) + jnp.dot(
        early_peer[0], late_peer, preferred_element_type=F32
    )
    out_part = jnp.dot(core_rows(rows_t, core), activated, preferred_element_type=F32) + jnp.dot(
        early_peer[1], activated_peer, preferred_element_type=F32
    )
    parts = jnp.concatenate([in_part.astype(BF16), out_part.astype(BF16)], axis=1)
    parts = lax.all_to_all(parts.reshape(32, 20, 1920), CHIPS, 0, 0)
    weights_sum = jnp.sum(parts.astype(F32), axis=0)
    grad_in = jnp.stack([weights_sum[:, :640], weights_sum[:, 640:1280]])
    grad_out = weights_sum[:, 1280:].T

    taps = kernel_part.reshape(64, -1)
    taps = jnp.sum(lax.all_to_all(taps, FRAMES, 0, 0), axis=0)
    taps = lax.all_to_all(jnp.broadcast_to(taps[None], (64, taps.shape[0])), FRAMES, 0, 0)
    grad_kernel = taps.reshape(kernel.shape)

    gains = lax.all_to_all(jnp.broadcast_to(gain_part[None], (128, gain_part.shape[0])), EVERY, 0, 0)
    grad_gain = jnp.sum(gains, axis=0)

    grad_normed = sent.astype(F32) + other.astype(F32)
    scaled_grad = grad_normed * norm_gain
    norm_back = inv_scale * (
        scaled_grad
        - jnp.mean(scaled_grad, axis=1, keepdims=True)
        - unit_frames * jnp.mean(scaled_grad * unit_frames, axis=1, keepdims=True)
    )
    grad_frames = (arrived.astype(F32) + norm_back).astype(BF16)
    return (grad_frames, grad_in, grad_out, grad_kernel, grad_gain)


def solution(mesh):
    split = Mesh(
        np.asarray(mesh.devices).reshape(2, 4, 2, 2, 4), ("xl", "y", "core", "tensor", "section")
    )
    outer = ("xl", "y", "core")
    in_specs = (
        P(FRAMES, None),
        P(outer, "section"),
        P(),
        P(None, None, "tensor"),
        P(None, "tensor"),
        P("tensor", None),
        P(),
        P(),
    )
    out_specs = (
        P(FRAMES, None),
        P(None, FRAMES, "tensor"),
        P("tensor", FRAMES),
        P(None, "tensor"),
        P(),
    )
    return jax.shard_map(body, mesh=split, in_specs=in_specs, out_specs=out_specs, check_vma=False)
```

```python
import functools

import jax
import jax.numpy as jnp
import numpy as np
from jax import lax
from jax.experimental import pallas as pl
from jax.experimental.pallas import tpu as pltpu
from jax.sharding import Mesh
from jax.sharding import PartitionSpec as P

BLOCK = 128
HALO = 16
TAPS = 31
LANES = 128
EPSILON = 1e-05
BF16 = jnp.bfloat16
F32 = jnp.float32

FRAMES = ("xl", "y", "core", "section")
PLANE = ("y", "section")
EVERY = ("xl", "y", "core", "tensor", "section")
VMEM_LIMIT = 48 * 1024 * 1024


def params():
    return pltpu.CompilerParams(vmem_limit_bytes=VMEM_LIMIT)


def cost(flops, moved, special=0):
    return pl.CostEstimate(flops=flops, bytes_accessed=moved, transcendentals=special)


def swap(value, axis):
    return lax.ppermute(value, axis, [(0, 1), (1, 0)])


def halos(shard):
    peers = lax.axis_size(FRAMES)
    up = [(i, i + 1) for i in range(peers - 1)]
    down = [(j, i) for i, j in up]
    before = lax.ppermute(shard[shard.shape[0] - HALO :], FRAMES, up)
    after = lax.ppermute(shard[:HALO], FRAMES, down)
    return before, after


def fill_windows(win, main, before, after, same):
    blocks = win.shape[0]
    for b in range(blocks):
        lo, hi = b * BLOCK, (b + 1) * BLOCK
        prior = before[...] if b == 0 else main[lo - HALO : lo, :]
        later = after[...] if b == blocks - 1 else main[hi : hi + HALO, :]
        win[b, HALO : HALO + BLOCK, :] = main[lo:hi, :].astype(F32)
        win[b, :HALO, :] = jnp.where(same[b] == 1, prior.astype(F32), 0.0)
        win[b, HALO + BLOCK :, :] = jnp.where(same[b + 1] == 1, later.astype(F32), 0.0)


def shifted(win, b, shift):
    first = 1 if shift == 0 else 0
    return [(8 * a + shift - 1, 8 * a) for a in range(first, 4)], win[b, pl.ds(shift, BLOCK + 24), :]


def convolve(win, b, taps, flip):
    total = jnp.zeros((BLOCK, LANES), F32)
    for shift in range(8):
        steps, rows = shifted(win, b, shift)
        for k, at in steps:
            row = TAPS - 1 - k if flip else k
            total = total + taps[row : row + 1, :] * rows[at : at + BLOCK]
    return total


def valid_rows(fill, b):
    return lax.broadcasted_iota(jnp.int32, (BLOCK, LANES), 0) < fill[b]


def forward_kernel(same, fill, units, before, after, taps, activated, slope, win):
    fill_windows(win, units, before, after, same)

    def step(b, carry):
        conv = convolve(win, b, taps, False)
        q = jax.nn.sigmoid(conv)
        valid = valid_rows(fill, b)
        rows = pl.ds(pl.multiple_of(b * BLOCK, BLOCK), BLOCK)
        activated[rows, :] = jnp.where(valid, conv * q, 0.0).astype(BF16)
        slope[rows, :] = jnp.where(valid, q + conv * q * (1.0 - q), 0.0)
        return carry

    lax.fori_loop(0, win.shape[0], step, 0)


def taps_kernel(same, units, before, after, grad_conv, out, win, sums):
    fill_windows(win, units, before, after, same)
    sums[...] = jnp.zeros_like(sums)

    def step(b, carry):
        grad = grad_conv[pl.ds(pl.multiple_of(b * BLOCK, BLOCK), BLOCK), :]
        for shift in range(8):
            steps, rows = shifted(win, b, shift)
            for k, at in steps:
                terms = (rows[at : at + BLOCK] * grad).reshape(BLOCK // 8, 8, LANES)
                sums[k] += jnp.sum(terms, axis=0)
        return carry

    lax.fori_loop(0, win.shape[0], step, 0)
    out[...] = jnp.sum(sums[...], axis=1)


def backward_kernel(same, fill, grad_conv, before, after, taps, value, gate, out, win):
    fill_windows(win, grad_conv, before, after, same)

    def step(b, carry):
        grad_units = jnp.where(valid_rows(fill, b), convolve(win, b, taps, True), 0.0)
        rows = pl.ds(pl.multiple_of(b * BLOCK, BLOCK), BLOCK)
        s = gate[rows, :]
        grad_value = grad_units * s
        out[0, rows, :] = grad_value.astype(BF16)
        out[1, rows, :] = (grad_value * value[rows, :] * (1.0 - s)).astype(BF16)
        return carry

    lax.fori_loop(0, win.shape[0], step, 0)


def normed_kernel(late, weights, frames, mean, inv, out, gain):
    contract = (((1,), (1,)), ((), ()))
    part = lax.dot_general(late[0], weights[0], contract, preferred_element_type=F32)
    part = part + lax.dot_general(late[1], weights[1], contract, preferred_element_type=F32)
    out[...] = part.astype(BF16)
    unit = (frames[...].astype(F32) - mean[...]) * inv[...]
    gain[...] = jnp.sum(part * unit, axis=0, keepdims=True)


def pair_kernel(left, left_peer, right, right_peer, out):
    total = jnp.dot(left[...], right[...], preferred_element_type=F32)
    total = total + jnp.dot(left_peer[...], right_peer[...], preferred_element_type=F32)
    out[...] = total.astype(BF16)


def smem():
    return pl.BlockSpec(memory_space=pltpu.SMEM)


def lanes(rows):
    return pl.BlockSpec((rows, LANES), lambda c: (0, c))


def convolved(same, fill, units, before, after, taps):
    count, width = units.shape
    return pl.pallas_call(
        forward_kernel,
        grid=(width // LANES,),
        in_specs=[smem(), smem(), lanes(count), lanes(HALO), lanes(HALO), lanes(TAPS)],
        out_specs=[lanes(count), lanes(count)],
        out_shape=[
            jax.ShapeDtypeStruct((count, width), BF16),
            jax.ShapeDtypeStruct((count, width), F32),
        ],
        scratch_shapes=[pltpu.VMEM((count // BLOCK, BLOCK + 2 * HALO, LANES), F32)],
        compiler_params=params(),
        cost_estimate=cost(2 * TAPS * count * width, 8 * count * width, count * width),
        name="conv_forward",
    )(same, fill, units, before, after, taps)


def tap_sums(same, units, before, after, grad_conv):
    count, width = units.shape
    return pl.pallas_call(
        taps_kernel,
        grid=(width // LANES,),
        in_specs=[smem(), lanes(count), lanes(HALO), lanes(HALO), lanes(count)],
        out_specs=lanes(32),
        out_shape=jax.ShapeDtypeStruct((32, width), F32),
        scratch_shapes=[
            pltpu.VMEM((count // BLOCK, BLOCK + 2 * HALO, LANES), F32),
            pltpu.VMEM((32, 8, LANES), F32),
        ],
        compiler_params=params(),
        cost_estimate=cost(2 * TAPS * count * width, 6 * count * width),
        name="tap_gradients",
    )(same, units, before, after, grad_conv)


def projected_back(same, fill, grad_conv, before, after, taps, value, gate):
    count, width = grad_conv.shape
    return pl.pallas_call(
        backward_kernel,
        grid=(width // LANES,),
        in_specs=[
            smem(),
            smem(),
            lanes(count),
            lanes(HALO),
            lanes(HALO),
            lanes(TAPS),
            lanes(count),
            lanes(count),
        ],
        out_specs=pl.BlockSpec((2, count, LANES), lambda c: (0, 0, c)),
        out_shape=jax.ShapeDtypeStruct((2, count, width), BF16),
        scratch_shapes=[pltpu.VMEM((count // BLOCK, BLOCK + 2 * HALO, LANES), F32)],
        compiler_params=params(),
        cost_estimate=cost(2 * TAPS * count * width, 16 * count * width),
        name="conv_backward",
    )(same, fill, grad_conv, before, after, taps, value, gate)


def normed_back(late, weights, frames, mean, inv):
    count, features = frames.shape
    width = late.shape[2]
    step = 256
    return pl.pallas_call(
        normed_kernel,
        grid=(features // step,),
        in_specs=[
            pl.BlockSpec((2, count, width), lambda d: (0, 0, 0)),
            pl.BlockSpec((2, step, width), lambda d: (0, d, 0)),
            pl.BlockSpec((count, step), lambda d: (0, d)),
            pl.BlockSpec((count, 1), lambda d: (0, 0)),
            pl.BlockSpec((count, 1), lambda d: (0, 0)),
        ],
        out_specs=[
            pl.BlockSpec((count, step), lambda d: (0, d)),
            pl.BlockSpec((1, step), lambda d: (0, d)),
        ],
        out_shape=[
            jax.ShapeDtypeStruct((count, features), BF16),
            jax.ShapeDtypeStruct((1, features), F32),
        ],
        compiler_params=params(),
        cost_estimate=cost(4 * count * width * features, 4 * (count + width) * features),
        name="normed_gradient",
    )(late, weights, frames, mean, inv)


def pair_product(left, left_peer, right, right_peer, step):
    rows, count = left.shape
    groups, _, width = right.shape
    halves = width // step
    spec = pl.BlockSpec((None, count, step), lambda i: (i // halves, 0, i % halves))
    whole = pl.BlockSpec((rows, count), lambda i: (0, 0))
    return pl.pallas_call(
        pair_kernel,
        grid=(groups * halves,),
        in_specs=[whole, whole, spec, spec],
        out_specs=pl.BlockSpec((rows, step), lambda i: (0, i)),
        out_shape=jax.ShapeDtypeStruct((rows, groups * width), BF16),
        compiler_params=params(),
        cost_estimate=cost(
            4 * rows * count * groups * width, 4 * count * (rows + groups * width) + 2 * rows * groups * width
        ),
        name="weight_gradient",
    )(left, left_peer, right, right_peer)


def row_table():
    table = np.zeros((2, 1280), np.int32)
    at = 0
    for half in range(2):
        for y in range(4):
            for z in range(4):
                for xl in range(2):
                    for r in range(20):
                        for core in range(2):
                            owner = core if half else 1 - core
                            table[core, at] = ((xl * 4 + y) * 2 + owner) * 80 + z * 20 + r
                        at += 1
    return table


def picked(selection, array):
    contract = (((1,), (1,)), ((), ()))
    return lax.dot_general(selection, array, contract, preferred_element_type=F32).astype(BF16)


def finish_rows(summed, xl):
    own = lax.dynamic_index_in_dim(summed, xl, 0, keepdims=False)
    other = lax.dynamic_index_in_dim(summed, 1 - xl, 0, keepdims=False)
    return own + swap(other, "xl")


def body(frames, returned, norm_gain, weight_in, kernel, weight_out, block_utt, block_fill):
    count = frames.shape[0]
    width = weight_in.shape[2]
    blocks = count // BLOCK
    core, xl = lax.axis_index("core"), lax.axis_index("xl")
    first_block = lax.axis_index(FRAMES) * blocks
    arrived = lax.all_to_all(returned, "section", split_axis=0, concat_axis=1, tiled=True)

    edge = jnp.full((1,), -1, jnp.int32)
    padded_utt = jnp.concatenate([edge, block_utt, edge])
    near_utt = lax.dynamic_slice(padded_utt, (first_block,), (blocks + 2,))
    same = (near_utt[1:] == near_utt[:-1]).astype(jnp.int32)
    fill = lax.dynamic_slice(block_fill, (first_block,), (blocks,))
    valid_frame = (jnp.arange(BLOCK, dtype=jnp.int32)[None, :] < fill[:, None]).reshape(-1)

    as_float = frames.astype(F32)
    mean = jnp.mean(as_float, axis=1, keepdims=True)
    center = as_float - mean
    inv_scale = lax.rsqrt(jnp.mean(center * center, axis=1, keepdims=True) + EPSILON)
    normed = (center * inv_scale * norm_gain).astype(BF16)
    value_proj = jnp.dot(normed, weight_in[0], preferred_element_type=F32)
    gate_proj = jnp.dot(normed, weight_in[1], preferred_element_type=F32)
    gate_sigmoid = jax.nn.sigmoid(gate_proj)
    gated_units = jnp.where(valid_frame[:, None], value_proj * gate_sigmoid, 0.0).astype(BF16)
    units_before, units_after = halos(gated_units)

    order = lax.dynamic_index_in_dim(jnp.asarray(row_table()), core, 0, keepdims=False)
    columns = lax.broadcasted_iota(jnp.int32, (1280, 1280), 1)
    selection = (order[:, None] == columns).astype(BF16)
    normed_t = picked(selection, normed)

    activated, slope = convolved(same, fill, gated_units, units_before, units_after, kernel)
    activated_peer = swap(activated, "core")
    normed_peer = swap(normed_t[:640], "core")

    grad_activated = lax.dot_general(
        arrived, weight_out, (((1,), (1,)), ((), ())), preferred_element_type=F32
    )
    grad_conv = grad_activated * slope
    conv_before, conv_after = halos(grad_conv)
    rows_t = picked(selection, arrived)
    rows_peer = swap(rows_t[:640], "core")
    taps_part = tap_sums(same, gated_units, units_before, units_after, grad_conv)
    out_part = pair_product(
        rows_t[640:], rows_peer, activated[None], activated_peer[None], width
    )
    out_send = jnp.concatenate(
        [
            out_part.reshape(16, 40, width),
            taps_part.astype(BF16).reshape(16, 2, width),
            jnp.zeros((16, 6, width), BF16),
        ],
        axis=1,
    )
    out_got = lax.all_to_all(out_send, PLANE, 0, 0)
    out_sum = jnp.sum(out_got.astype(F32), axis=0)
    grad_out = finish_rows(out_sum[:40].reshape(2, 20, width), xl).T

    late = projected_back(
        same, fill, grad_conv, conv_before, conv_after, kernel, value_proj, gate_sigmoid
    )
    late_peer = swap(late, "core")
    sent, gain_part = normed_back(late, weight_in, frames, mean, inv_scale)
    other = swap(sent, "tensor")
    in_part = pair_product(normed_t[640:], normed_peer, late, late_peer, width)
    in_got = lax.all_to_all(in_part.reshape(16, 40, 2 * width), PLANE, 0, 0)
    in_sum = finish_rows(jnp.sum(in_got.astype(F32), axis=0).reshape(2, 20, 2 * width), xl)
    grad_in = jnp.stack([in_sum[:, :width], in_sum[:, width:]])

    tap_rows = out_sum[40:42].reshape(1, 2 * width)
    small = jnp.concatenate([tap_rows, gain_part], axis=1).astype(BF16)
    small = lax.all_to_all(jnp.broadcast_to(small, (128, small.shape[1])), EVERY, 0, 0)
    grad_gain = jnp.sum(small[:, 2 * width :].astype(F32), axis=0)
    tensor = lax.axis_index("tensor")
    tap_shares = small[:, : 2 * width].reshape(2, 4, 2, 2, 4, 2, width)
    tap_shares = lax.dynamic_index_in_dim(tap_shares, tensor, 3, keepdims=False)
    grad_kernel = jnp.sum(tap_shares.astype(F32), axis=(0, 2)).reshape(32, width)[:TAPS]

    grad_normed = sent.astype(F32) + other.astype(F32)
    scaled_grad = grad_normed * norm_gain
    unit_frames = center * inv_scale
    norm_back = inv_scale * (
        scaled_grad
        - jnp.mean(scaled_grad, axis=1, keepdims=True)
        - unit_frames * jnp.mean(scaled_grad * unit_frames, axis=1, keepdims=True)
    )
    grad_frames = (arrived.astype(F32) + norm_back).astype(BF16)
    return (grad_frames, grad_in, grad_out, grad_kernel, grad_gain)


def solution(mesh):
    split = Mesh(
        np.asarray(mesh.devices).reshape(2, 4, 2, 2, 4), ("xl", "y", "core", "tensor", "section")
    )
    outer = ("xl", "y", "core")
    in_specs = (
        P(FRAMES, None),
        P(outer, "section"),
        P(),
        P(None, None, "tensor"),
        P(None, "tensor"),
        P("tensor", None),
        P(),
        P(),
    )
    out_specs = (
        P(FRAMES, None),
        P(None, FRAMES, "tensor"),
        P("tensor", FRAMES),
        P(None, "tensor"),
        P(),
    )
    return jax.shard_map(body, mesh=split, in_specs=in_specs, out_specs=out_specs, check_vma=False)
```

```python
import functools

import jax
import jax.numpy as jnp
import numpy as np
from jax import lax
from jax.experimental import pallas as pl
from jax.experimental.pallas import tpu as pltpu
from jax.sharding import Mesh
from jax.sharding import PartitionSpec as P

BLOCK = 128
HALO = 16
TAPS = 31
LANES = 128
EPSILON = 1e-05
BF16 = jnp.bfloat16
F32 = jnp.float32

FRAMES = ("xl", "y", "core", "section")
PLANE = ("y", "section")
MIB = 1024 * 1024


def params(mib=16):
    return pltpu.CompilerParams(vmem_limit_bytes=mib * MIB)


def in_hbm(array):
    return pltpu.with_memory_space_constraint(array, pltpu.HBM)


def swap(value, axis):
    return lax.ppermute(value, axis, [(0, 1), (1, 0)])


def halos(shard):
    peers = lax.axis_size(FRAMES)
    up = [(i, i + 1) for i in range(peers - 1)]
    down = [(j, i) for i, j in up]
    before = lax.ppermute(shard[shard.shape[0] - HALO :], FRAMES, up)
    after = lax.ppermute(shard[:HALO], FRAMES, down)
    return before, after


def fill_windows(win, main, before, after, same):
    blocks = win.shape[0]
    for b in range(blocks):
        lo, hi = b * BLOCK, (b + 1) * BLOCK
        prior = before[...] if b == 0 else main[lo - HALO : lo, :]
        later = after[...] if b == blocks - 1 else main[hi : hi + HALO, :]
        win[b, HALO : HALO + BLOCK, :] = main[lo:hi, :].astype(F32)
        win[b, :HALO, :] = jnp.where(same[b] == 1, prior.astype(F32), 0.0)
        win[b, HALO + BLOCK :, :] = jnp.where(same[b + 1] == 1, later.astype(F32), 0.0)


def fill_extended(win, rows, same):
    for b in range(win.shape[0]):
        lo = b * BLOCK
        hi = lo + HALO + BLOCK
        win[b, HALO : HALO + BLOCK, :] = rows[lo + HALO : hi, :].astype(F32)
        win[b, :HALO, :] = jnp.where(same[b] == 1, rows[lo : lo + HALO, :].astype(F32), 0.0)
        win[b, HALO + BLOCK :, :] = jnp.where(same[b + 1] == 1, rows[hi : hi + HALO, :].astype(F32), 0.0)


def shifted(win, b, shift):
    first = 1 if shift == 0 else 0
    return [(8 * a + shift - 1, 8 * a) for a in range(first, 4)], win[b, pl.ds(shift, BLOCK + 24), :]


def convolve(win, b, taps, flip):
    total = jnp.zeros((BLOCK, LANES), F32)
    for shift in range(8):
        steps, rows = shifted(win, b, shift)
        for k, at in steps:
            row = TAPS - 1 - k if flip else k
            total = total + taps[row : row + 1, :] * rows[at : at + BLOCK]
    return total


def valid_rows(fill, b):
    return lax.broadcasted_iota(jnp.int32, (BLOCK, LANES), 0) < fill[b]


def forward_kernel(same, fill, units, taps, activated, slope, win):
    fill_extended(win, units, same)

    def step(b, carry):
        conv = convolve(win, b, taps, False)
        q = jax.nn.sigmoid(conv)
        valid = valid_rows(fill, b)
        rows = pl.ds(pl.multiple_of(b * BLOCK, BLOCK), BLOCK)
        activated[rows, :] = jnp.where(valid, conv * q, 0.0).astype(BF16)
        slope[rows, :] = jnp.where(valid, q + conv * q * (1.0 - q), 0.0)
        return carry

    lax.fori_loop(0, win.shape[0], step, 0)


def taps_kernel(same, units, grad_conv, out, win, sums):
    fill_extended(win, units, same)
    sums[...] = jnp.zeros_like(sums)

    def step(b, carry):
        grad = grad_conv[pl.ds(pl.multiple_of(b * BLOCK, BLOCK), BLOCK), :]
        for shift in range(8):
            steps, rows = shifted(win, b, shift)
            for k, at in steps:
                terms = (rows[at : at + BLOCK] * grad).reshape(BLOCK // 8, 8, LANES)
                sums[k] += jnp.sum(terms, axis=0)
        return carry

    lax.fori_loop(0, win.shape[0], step, 0)
    out[...] = jnp.sum(sums[...], axis=1)


def backward_kernel(same, fill, grad_conv, before, after, taps, value, gate, out, win):
    fill_windows(win, grad_conv, before, after, same)

    def step(b, carry):
        grad_units = jnp.where(valid_rows(fill, b), convolve(win, b, taps, True), 0.0)
        rows = pl.ds(pl.multiple_of(b * BLOCK, BLOCK), BLOCK)
        inner = pl.ds(pl.multiple_of(b * BLOCK + HALO, HALO), BLOCK)
        s = gate[inner, :]
        grad_value = grad_units * s
        out[0, rows, :] = grad_value.astype(BF16)
        out[1, rows, :] = (grad_value * value[inner, :] * (1.0 - s)).astype(BF16)
        return carry

    lax.fori_loop(0, win.shape[0], step, 0)


def norm_kernel(frames, before, after, gain, out, out_t):
    def rows(block):
        x = block.astype(F32)
        center = x - jnp.mean(x, axis=1, keepdims=True)
        inv = lax.rsqrt(jnp.mean(center * center, axis=1, keepdims=True) + EPSILON)
        return (center * inv * gain[...]).astype(BF16)

    i = pl.program_id(0)
    normed = rows(frames[...])
    out[pl.ds(pl.multiple_of(HALO + i * BLOCK, HALO), BLOCK), :] = normed
    out_t[...] = normed.T

    @pl.when(i == 0)
    def _():
        out[:HALO, :] = rows(before[...])
        out[out.shape[0] - HALO :, :] = rows(after[...])


def chunks_kernel(rows, out, held, sems):
    count = held.shape[2]
    parts = range(held.shape[0])
    loads = [pltpu.make_async_copy(rows.at[:, pl.ds(i * count, count)], held.at[i], sems.at[0, i]) for i in parts]
    stores = [pltpu.make_async_copy(held.at[i], out.at[i], sems.at[1, i]) for i in parts]
    for load in loads:
        load.start()
    for load, store in zip(loads, stores):
        load.wait()
        store.start()
    for store in stores:
        store.wait()


def halves_kernel(core, rows, order, own, other, held, sem):
    copy = pltpu.make_async_copy(held, other, sem)
    for half, out in ((1 - core[0], held), (core[0], own)):
        for y in range(4):
            first = pl.multiple_of(y * 160 + half * 80, 16)
            second = pl.multiple_of((4 + y) * 160 + half * 80, 16)
            both = jnp.concatenate([rows[pl.ds(first, 80), :], rows[pl.ds(second, 80), :]], axis=0)
            moved = jnp.dot(order[...], both, preferred_element_type=F32)
            out[y * 160 : (y + 1) * 160, :] = moved.astype(BF16)
        if out is held:
            copy.start()
    copy.wait()


def final_kernel(sent, other, frames, arrived, gain, out, gain_part):
    x = frames[...].astype(F32)
    center = x - jnp.mean(x, axis=1, keepdims=True)
    inv = lax.rsqrt(jnp.mean(center * center, axis=1, keepdims=True) + EPSILON)
    unit = center * inv
    grad = sent[...].astype(F32) + other[...].astype(F32)
    e = grad * gain[...]
    product = grad * unit
    back = e - jnp.mean(e, axis=1, keepdims=True) - unit * jnp.mean(product * gain[...], axis=1, keepdims=True)
    out[...] = (arrived[...].astype(F32).T + inv * back).astype(BF16)

    @pl.when(pl.program_id(0) == 0)
    def _():
        gain_part[...] = jnp.zeros_like(gain_part)

    gain_part[...] += jnp.sum(product, axis=0, keepdims=True)


def pair_kernel(left, left_peer, right, right_peer, *buffers):
    out = buffers[-1]
    total = jnp.dot(left[...], right[...], preferred_element_type=F32)
    total = total + jnp.dot(left_peer[...], right_peer[...], preferred_element_type=F32)
    out[...] = total.astype(BF16)


def hbm():
    return pl.BlockSpec(memory_space=pltpu.HBM)


def smem():
    return pl.BlockSpec(memory_space=pltpu.SMEM)


def lanes(rows):
    return pl.BlockSpec((rows, LANES), lambda c: (0, c))


def convolved(same, fill, units, taps, count):
    width = units.shape[1]
    return pl.pallas_call(
        forward_kernel,
        grid=(width // LANES,),
        in_specs=[smem(), smem(), lanes(units.shape[0]), lanes(TAPS)],
        out_specs=[lanes(count), lanes(count)],
        out_shape=[
            jax.ShapeDtypeStruct((count, width), BF16),
            jax.ShapeDtypeStruct((count, width), F32),
        ],
        scratch_shapes=[pltpu.VMEM((count // BLOCK, BLOCK + 2 * HALO, LANES), F32)],
        compiler_params=params(),
        cost_estimate=pl.CostEstimate(flops=0, bytes_accessed=0, transcendentals=0),
        name="conv_forward",
    )(same, fill, units, taps)


def tap_sums(same, units, grad_conv):
    count, width = grad_conv.shape
    return pl.pallas_call(
        taps_kernel,
        grid=(width // LANES,),
        in_specs=[smem(), lanes(units.shape[0]), lanes(count)],
        out_specs=lanes(32),
        out_shape=jax.ShapeDtypeStruct((32, width), F32),
        scratch_shapes=[
            pltpu.VMEM((count // BLOCK, BLOCK + 2 * HALO, LANES), F32),
            pltpu.VMEM((32, 8, LANES), F32),
        ],
        compiler_params=params(),
        name="tap_gradients",
    )(same, units, grad_conv)


def projected_back(same, fill, grad_conv, before, after, taps, value, gate):
    count, width = grad_conv.shape
    return pl.pallas_call(
        backward_kernel,
        grid=(width // LANES,),
        in_specs=[
            smem(),
            smem(),
            lanes(count),
            lanes(HALO),
            lanes(HALO),
            lanes(TAPS),
            lanes(value.shape[0]),
            lanes(value.shape[0]),
        ],
        out_specs=pl.BlockSpec((2, count, LANES), lambda c: (0, 0, c)),
        out_shape=jax.ShapeDtypeStruct((2, count, width), BF16),
        scratch_shapes=[pltpu.VMEM((count // BLOCK, BLOCK + 2 * HALO, LANES), F32)],
        compiler_params=params(),
        name="conv_backward",
    )(same, fill, grad_conv, before, after, taps, in_hbm(value), in_hbm(gate))


def normalised(frames, before, after, gain):
    count, features = frames.shape
    edge = pl.BlockSpec((HALO, features), lambda i: (0, 0))
    return pl.pallas_call(
        norm_kernel,
        grid=(count // BLOCK,),
        in_specs=[
            pl.BlockSpec((BLOCK, features), lambda i: (i, 0)),
            edge,
            edge,
            pl.BlockSpec((1, features), lambda i: (0, 0)),
        ],
        out_specs=[
            pl.BlockSpec((count + 2 * HALO, features), lambda i: (0, 0)),
            pl.BlockSpec((features, BLOCK), lambda i: (0, i)),
        ],
        out_shape=[
            jax.ShapeDtypeStruct((count + 2 * HALO, features), BF16),
            jax.ShapeDtypeStruct((features, count), BF16),
        ],
        compiler_params=params(),
        name="layer_norm",
    )(in_hbm(frames), before, after, gain.reshape(1, features))


def frame_chunks(rows, parts):
    features, total = rows.shape
    shape = (parts, features, total // parts)
    return pl.pallas_call(
        chunks_kernel,
        in_specs=[hbm()],
        out_specs=hbm(),
        out_shape=pltpu.HBM(shape, rows.dtype),
        scratch_shapes=[pltpu.VMEM(shape, rows.dtype), pltpu.SemaphoreType.DMA((2, parts))],
        compiler_params=params(),
        name="frame_chunks",
    )(in_hbm(rows))


def halves(core, rows):
    features, count = rows.shape
    order = np.zeros((160, 160), np.float32)
    for z in range(4):
        for x in range(2):
            for r in range(20):
                order[(z * 2 + x) * 20 + r, x * 80 + z * 20 + r] = 1.0
    vmem = pl.BlockSpec(memory_space=pltpu.VMEM)
    half = jax.ShapeDtypeStruct((features // 2, count), BF16)
    return pl.pallas_call(
        halves_kernel,
        in_specs=[smem(), vmem, vmem],
        out_specs=[vmem, hbm()],
        out_shape=[half, pltpu.HBM(half.shape, BF16)],
        scratch_shapes=[pltpu.VMEM(half.shape, BF16), pltpu.SemaphoreType.DMA],
        compiler_params=params(),
        name="core_halves",
    )(core.reshape(1), rows, jnp.asarray(order, BF16))


def norm_back(sent, other, frames, arrived, gain):
    count, features = frames.shape
    block = pl.BlockSpec((BLOCK, features), lambda i: (i, 0))
    return pl.pallas_call(
        final_kernel,
        grid=(count // BLOCK,),
        in_specs=[
            block,
            block,
            block,
            pl.BlockSpec((features, BLOCK), lambda i: (0, i)),
            pl.BlockSpec((1, features), lambda i: (0, 0)),
        ],
        out_specs=[block, pl.BlockSpec((1, features), lambda i: (0, 0))],
        out_shape=[jax.ShapeDtypeStruct((count, features), BF16), jax.ShapeDtypeStruct((1, features), F32)],
        compiler_params=params(),
        cost_estimate=pl.CostEstimate(flops=40_000_000_000, bytes_accessed=100_000_000, transcendentals=0),
        name="norm_backward",
    )(in_hbm(sent), in_hbm(other), in_hbm(frames), in_hbm(arrived), gain)


def pair_product(left, left_peer, right, right_peer, groups, first, buffer=None):
    rows, count = left.shape
    made, _, width = right.shape
    spec = pl.BlockSpec((None, count, width), lambda i: (i, 0, 0))
    whole = pl.BlockSpec((rows, count), lambda i: (0, 0))
    return pl.pallas_call(
        pair_kernel,
        grid=(made,),
        in_specs=[whole, whole, spec, spec] + ([] if buffer is None else [hbm()]),
        out_specs=pl.BlockSpec((rows, width), lambda i: (0, first + i)),
        out_shape=pltpu.HBM((rows, groups * width), BF16),
        input_output_aliases={} if buffer is None else {4: 0},
        compiler_params=params(),
        name="weight_gradient",
    )(left, left_peer, right, right_peer, *([] if buffer is None else [in_hbm(buffer)]))


def ring_shares(value, axis):
    return [value] + [lax.ppermute(value, axis, [(i, (i + by) % 4) for i in range(4)]) for by in (1, 2, 3)]


def ring_sum(shares):
    own, first, second, third = [share.astype(F32) for share in shares]
    return (own + second) + (first + third)


def finish_rows(summed, xl):
    own = lax.dynamic_index_in_dim(summed, xl, 0, keepdims=False)
    other = lax.dynamic_index_in_dim(summed, 1 - xl, 0, keepdims=False)
    return own + swap(other, "xl")


def body(frames, returned, norm_gain, weight_in, kernel, weight_out, block_utt, block_fill):
    count = frames.shape[0]
    width = weight_in.shape[2]
    features = frames.shape[1]
    blocks = count // BLOCK
    core, xl = lax.axis_index("core"), lax.axis_index("xl")
    first_block = lax.axis_index(FRAMES) * blocks
    frames_before, frames_after = halos(frames)
    chunks = frame_chunks(returned.T, 4)
    arrived = lax.all_to_all(chunks, "section", 0, 0).reshape(features, count)

    edge = jnp.full((1,), -1, jnp.int32)
    near_utt = lax.dynamic_slice(jnp.concatenate([edge, block_utt, edge]), (first_block,), (blocks + 2,))
    near_fill = lax.dynamic_slice(jnp.concatenate([edge, block_fill, edge]), (first_block,), (blocks + 2,))
    same = (near_utt[1:] == near_utt[:-1]).astype(jnp.int32)
    fill = near_fill[1:-1]
    valid = (jnp.arange(BLOCK, dtype=jnp.int32)[None, :] < near_fill[:, None]).reshape(-1)
    valid = valid[BLOCK - HALO : BLOCK + count + HALO]

    normed_ext, normed_t = normalised(frames, frames_before, frames_after, norm_gain)
    value_proj = jnp.dot(normed_ext, weight_in[0], preferred_element_type=F32)
    gate_proj = jnp.dot(normed_ext, weight_in[1], preferred_element_type=F32)
    gate_sigmoid = jax.nn.sigmoid(gate_proj)
    units = jnp.where(valid[:, None], value_proj * gate_sigmoid, 0.0).astype(BF16)
    activated, slope = convolved(same, fill, units, kernel, count)
    activated_peer = swap(activated, "core")

    normed_own, normed_other = halves(core, normed_t)
    normed_peer = swap(normed_other, "core")

    arrived, normed_own, normed_other = lax.optimization_barrier((arrived, normed_own, normed_other))
    grad_activated = lax.dot_general(
        arrived, weight_out, (((0,), (1,)), ((), ())), preferred_element_type=F32
    )
    grad_conv = grad_activated * slope
    conv_before, conv_after = halos(grad_conv)
    rows_own, rows_other = halves(core, arrived)
    rows_peer = swap(rows_other, "core")
    parts = pair_product(rows_own, rows_peer, activated[None], activated_peer[None], 3, 0)

    ready, parts = lax.optimization_barrier((grad_conv, parts))
    late = projected_back(
        same, fill, ready, conv_before, conv_after, kernel, value_proj, gate_sigmoid
    )
    late_peer = swap(late, "core")
    contract = (((1,), (1,)), ((), ()))
    sent = lax.dot_general(late[0], weight_in[0], contract, preferred_element_type=F32)
    sent = sent + lax.dot_general(late[1], weight_in[1], contract, preferred_element_type=F32)
    sent = sent.astype(BF16)
    other = swap(sent, "tensor")
    parts = pair_product(normed_own, normed_peer, late, late_peer, 3, 1, parts)
    got = lax.all_to_all(parts.reshape(16, 40, 3 * width), PLANE, 0, 0)

    grad_frames, gain_part = norm_back(sent, other, frames, arrived, norm_gain.reshape(1, features))
    ready, gain_part = lax.optimization_barrier((grad_conv, gain_part))
    taps_part = tap_sums(same, units, ready)
    small = jnp.concatenate([taps_part, gain_part.reshape(2, width)], axis=0)
    small = small + swap(small, "core")
    small = (small + swap(small, "xl")).astype(BF16)
    shares = ring_shares(small, "y")
    total = jnp.sum(got.astype(F32), axis=0)
    total, shares = lax.optimization_barrier((total, shares))
    summed = finish_rows(total.reshape(2, 20, 3 * width), xl)
    small = ring_sum(ring_shares(ring_sum(shares).astype(BF16), "section"))
    grad_kernel = small[:TAPS]
    grad_gain = small[32:].reshape(features)

    grad_out = summed[:, :width].T
    grad_in = jnp.stack([summed[:, width : 2 * width], summed[:, 2 * width :]])
    return (grad_frames, grad_in, grad_out, grad_kernel, grad_gain)


def solution(mesh):
    split = Mesh(
        np.asarray(mesh.devices).reshape(2, 4, 2, 2, 4), ("xl", "y", "core", "tensor", "section")
    )
    outer = ("xl", "y", "core")
    in_specs = (
        P(FRAMES, None),
        P(outer, "section"),
        P(),
        P(None, None, "tensor"),
        P(None, "tensor"),
        P("tensor", None),
        P(),
        P(),
    )
    out_specs = (
        P(FRAMES, None),
        P(None, FRAMES, "tensor"),
        P("tensor", FRAMES),
        P(None, "tensor"),
        P(),
    )
    return jax.shard_map(body, mesh=split, in_specs=in_specs, out_specs=out_specs, check_vma=False)
```

```python
import functools

import jax
import jax.numpy as jnp
import numpy as np
from jax import lax
from jax.experimental import pallas as pl
from jax.experimental.pallas import tpu as pltpu
from jax.sharding import Mesh
from jax.sharding import PartitionSpec as P

BLOCK = 128
HALO = 16
TAPS = 31
LANES = 128
EPSILON = 1e-05
BF16 = jnp.bfloat16
F32 = jnp.float32

FRAMES = ("xl", "y", "core", "section")
PLANE = ("y", "section")
MIB = 1024 * 1024


def params(mib=16):
    return pltpu.CompilerParams(vmem_limit_bytes=mib * MIB)


def in_hbm(array):
    return pltpu.with_memory_space_constraint(array, pltpu.HBM)


def swap(value, axis):
    return lax.ppermute(value, axis, [(0, 1), (1, 0)])


def halos(shard):
    peers = lax.axis_size(FRAMES)
    up = [(i, i + 1) for i in range(peers - 1)]
    down = [(j, i) for i, j in up]
    before = lax.ppermute(shard[shard.shape[0] - HALO :], FRAMES, up)
    after = lax.ppermute(shard[:HALO], FRAMES, down)
    return before, after


def fill_windows(win, main, before, after, same):
    blocks = win.shape[0]
    for b in range(blocks):
        lo, hi = b * BLOCK, (b + 1) * BLOCK
        prior = before[...] if b == 0 else main[lo - HALO : lo, :]
        later = after[...] if b == blocks - 1 else main[hi : hi + HALO, :]
        win[b, HALO : HALO + BLOCK, :] = main[lo:hi, :].astype(F32)
        win[b, :HALO, :] = jnp.where(same[b] == 1, prior.astype(F32), 0.0)
        win[b, HALO + BLOCK :, :] = jnp.where(same[b + 1] == 1, later.astype(F32), 0.0)


def fill_extended(win, rows, same):
    for b in range(win.shape[0]):
        lo = b * BLOCK
        hi = lo + HALO + BLOCK
        win[b, HALO : HALO + BLOCK, :] = rows[lo + HALO : hi, :].astype(F32)
        win[b, :HALO, :] = jnp.where(same[b] == 1, rows[lo : lo + HALO, :].astype(F32), 0.0)
        win[b, HALO + BLOCK :, :] = jnp.where(same[b + 1] == 1, rows[hi : hi + HALO, :].astype(F32), 0.0)


def shifted(win, b, shift):
    first = 1 if shift == 0 else 0
    return [(8 * a + shift - 1, 8 * a) for a in range(first, 4)], win[b, pl.ds(shift, BLOCK + 24), :]


def convolve(win, b, taps, flip):
    total = jnp.zeros((BLOCK, LANES), F32)
    for shift in range(8):
        steps, rows = shifted(win, b, shift)
        for k, at in steps:
            row = TAPS - 1 - k if flip else k
            total = total + taps[row : row + 1, :] * rows[at : at + BLOCK]
    return total


def valid_rows(fill, b):
    return lax.broadcasted_iota(jnp.int32, (BLOCK, LANES), 0) < fill[b]


def forward_kernel(same, fill, units, taps, activated, slope, win):
    fill_extended(win, units, same)

    def step(b, carry):
        conv = convolve(win, b, taps, False)
        q = jax.nn.sigmoid(conv)
        valid = valid_rows(fill, b)
        rows = pl.ds(pl.multiple_of(b * BLOCK, BLOCK), BLOCK)
        activated[rows, :] = jnp.where(valid, conv * q, 0.0).astype(BF16)
        slope[rows, :] = jnp.where(valid, q + conv * q * (1.0 - q), 0.0)
        return carry

    lax.fori_loop(0, win.shape[0], step, 0)


def taps_kernel(same, units, grad_conv, out, win, sums):
    fill_extended(win, units, same)
    sums[...] = jnp.zeros_like(sums)

    def step(b, carry):
        grad = grad_conv[pl.ds(pl.multiple_of(b * BLOCK, BLOCK), BLOCK), :]
        for shift in range(8):
            steps, rows = shifted(win, b, shift)
            for k, at in steps:
                terms = (rows[at : at + BLOCK] * grad).reshape(BLOCK // 8, 8, LANES)
                sums[k] += jnp.sum(terms, axis=0)
        return carry

    lax.fori_loop(0, win.shape[0], step, 0)
    out[...] = jnp.sum(sums[...], axis=1)


def backward_kernel(same, fill, grad_conv, before, after, taps, value, gate, out, win):
    fill_windows(win, grad_conv, before, after, same)

    def step(b, carry):
        grad_units = jnp.where(valid_rows(fill, b), convolve(win, b, taps, True), 0.0)
        rows = pl.ds(pl.multiple_of(b * BLOCK, BLOCK), BLOCK)
        inner = pl.ds(pl.multiple_of(b * BLOCK + HALO, HALO), BLOCK)
        s = gate[inner, :]
        grad_value = grad_units * s
        out[0, rows, :] = grad_value.astype(BF16)
        out[1, rows, :] = (grad_value * value[inner, :] * (1.0 - s)).astype(BF16)
        return carry

    lax.fori_loop(0, win.shape[0], step, 0)


def norm_kernel(frames, before, after, gain, out, out_t):
    def rows(block):
        x = block.astype(F32)
        center = x - jnp.mean(x, axis=1, keepdims=True)
        inv = lax.rsqrt(jnp.mean(center * center, axis=1, keepdims=True) + EPSILON)
        return (center * inv * gain[...]).astype(BF16)

    i = pl.program_id(0)
    normed = rows(frames[...])
    out[pl.ds(pl.multiple_of(HALO + i * BLOCK, HALO), BLOCK), :] = normed
    out_t[...] = normed.T

    @pl.when(i == 0)
    def _():
        out[:HALO, :] = rows(before[...])
        out[out.shape[0] - HALO :, :] = rows(after[...])


def chunks_kernel(rows, out, held, sems):
    count = held.shape[2]
    parts = range(held.shape[0])
    loads = [pltpu.make_async_copy(rows.at[:, pl.ds(i * count, count)], held.at[i], sems.at[0, i]) for i in parts]
    stores = [pltpu.make_async_copy(held.at[i], out.at[i], sems.at[1, i]) for i in parts]
    for load in loads:
        load.start()
    for load, store in zip(loads, stores):
        load.wait()
        store.start()
    for store in stores:
        store.wait()


def halves_kernel(core, rows, order, own, other, held, sem):
    copy = pltpu.make_async_copy(held, other, sem)
    for half, out in ((1 - core[0], held), (core[0], own)):
        for y in range(4):
            first = pl.multiple_of(y * 160 + half * 80, 16)
            second = pl.multiple_of((4 + y) * 160 + half * 80, 16)
            both = jnp.concatenate([rows[pl.ds(first, 80), :], rows[pl.ds(second, 80), :]], axis=0)
            moved = jnp.dot(order[...], both, preferred_element_type=F32)
            out[y * 160 : (y + 1) * 160, :] = moved.astype(BF16)
        if out is held:
            copy.start()
    copy.wait()


def final_kernel(sent, other, frames, arrived, gain, out):
    x = frames[...].astype(F32)
    center = x - jnp.mean(x, axis=1, keepdims=True)
    inv = lax.rsqrt(jnp.mean(center * center, axis=1, keepdims=True) + EPSILON)
    unit = center * inv
    e = (sent[...].astype(F32) + other[...].astype(F32)) * gain[...]
    back = e - jnp.mean(e, axis=1, keepdims=True) - unit * jnp.mean(e * unit, axis=1, keepdims=True)
    out[...] = (arrived[...].astype(F32).T + inv * back).astype(BF16)


def pair_kernel(left, left_peer, right, right_peer, *buffers):
    out = buffers[-1]
    total = jnp.dot(left[...], right[...], preferred_element_type=F32)
    total = total + jnp.dot(left_peer[...], right_peer[...], preferred_element_type=F32)
    out[...] = total.astype(BF16)


def hbm():
    return pl.BlockSpec(memory_space=pltpu.HBM)


def smem():
    return pl.BlockSpec(memory_space=pltpu.SMEM)


def lanes(rows):
    return pl.BlockSpec((rows, LANES), lambda c: (0, c))


def convolved(same, fill, units, taps, count):
    width = units.shape[1]
    return pl.pallas_call(
        forward_kernel,
        grid=(width // LANES,),
        in_specs=[smem(), smem(), lanes(units.shape[0]), lanes(TAPS)],
        out_specs=[lanes(count), lanes(count)],
        out_shape=[
            jax.ShapeDtypeStruct((count, width), BF16),
            jax.ShapeDtypeStruct((count, width), F32),
        ],
        scratch_shapes=[pltpu.VMEM((count // BLOCK, BLOCK + 2 * HALO, LANES), F32)],
        compiler_params=params(),
        cost_estimate=pl.CostEstimate(flops=0, bytes_accessed=0, transcendentals=0),
        name="conv_forward",
    )(same, fill, units, taps)


def tap_sums(same, units, grad_conv):
    count, width = grad_conv.shape
    return pl.pallas_call(
        taps_kernel,
        grid=(width // LANES,),
        in_specs=[smem(), lanes(units.shape[0]), lanes(count)],
        out_specs=lanes(32),
        out_shape=jax.ShapeDtypeStruct((32, width), F32),
        scratch_shapes=[
            pltpu.VMEM((count // BLOCK, BLOCK + 2 * HALO, LANES), F32),
            pltpu.VMEM((32, 8, LANES), F32),
        ],
        compiler_params=params(),
        cost_estimate=pl.CostEstimate(flops=1_000_000, bytes_accessed=0, transcendentals=0),
        name="tap_gradients",
    )(same, units, grad_conv)


def projected_back(same, fill, grad_conv, before, after, taps, value, gate):
    count, width = grad_conv.shape
    return pl.pallas_call(
        backward_kernel,
        grid=(width // LANES,),
        in_specs=[
            smem(),
            smem(),
            lanes(count),
            lanes(HALO),
            lanes(HALO),
            lanes(TAPS),
            lanes(value.shape[0]),
            lanes(value.shape[0]),
        ],
        out_specs=pl.BlockSpec((2, count, LANES), lambda c: (0, 0, c)),
        out_shape=jax.ShapeDtypeStruct((2, count, width), BF16),
        scratch_shapes=[pltpu.VMEM((count // BLOCK, BLOCK + 2 * HALO, LANES), F32)],
        compiler_params=params(),
        name="conv_backward",
    )(same, fill, grad_conv, before, after, taps, in_hbm(value), in_hbm(gate))


def normalised(frames, before, after, gain):
    count, features = frames.shape
    edge = pl.BlockSpec((HALO, features), lambda i: (0, 0))
    return pl.pallas_call(
        norm_kernel,
        grid=(count // BLOCK,),
        in_specs=[
            pl.BlockSpec((BLOCK, features), lambda i: (i, 0)),
            edge,
            edge,
            pl.BlockSpec((1, features), lambda i: (0, 0)),
        ],
        out_specs=[
            pl.BlockSpec((count + 2 * HALO, features), lambda i: (0, 0)),
            pl.BlockSpec((features, BLOCK), lambda i: (0, i)),
        ],
        out_shape=[
            jax.ShapeDtypeStruct((count + 2 * HALO, features), BF16),
            jax.ShapeDtypeStruct((features, count), BF16),
        ],
        compiler_params=params(),
        name="layer_norm",
    )(in_hbm(frames), before, after, gain.reshape(1, features))


def frame_chunks(rows, parts):
    features, total = rows.shape
    shape = (parts, features, total // parts)
    return pl.pallas_call(
        chunks_kernel,
        in_specs=[hbm()],
        out_specs=hbm(),
        out_shape=pltpu.HBM(shape, rows.dtype),
        scratch_shapes=[pltpu.VMEM(shape, rows.dtype), pltpu.SemaphoreType.DMA((2, parts))],
        compiler_params=params(),
        name="frame_chunks",
    )(in_hbm(rows))


def halves(core, rows):
    features, count = rows.shape
    order = np.zeros((160, 160), np.float32)
    for z in range(4):
        for x in range(2):
            for r in range(20):
                order[(z * 2 + x) * 20 + r, x * 80 + z * 20 + r] = 1.0
    vmem = pl.BlockSpec(memory_space=pltpu.VMEM)
    half = jax.ShapeDtypeStruct((features // 2, count), BF16)
    return pl.pallas_call(
        halves_kernel,
        in_specs=[smem(), vmem, vmem],
        out_specs=[vmem, hbm()],
        out_shape=[half, pltpu.HBM(half.shape, BF16)],
        scratch_shapes=[pltpu.VMEM(half.shape, BF16), pltpu.SemaphoreType.DMA],
        compiler_params=params(),
        name="core_halves",
    )(core.reshape(1), rows, jnp.asarray(order, BF16))


def norm_back(sent, other, frames, arrived, gain):
    count, features = frames.shape
    block = pl.BlockSpec((BLOCK, features), lambda i: (i, 0))
    return pl.pallas_call(
        final_kernel,
        grid=(count // BLOCK,),
        in_specs=[
            block,
            block,
            block,
            pl.BlockSpec((features, BLOCK), lambda i: (0, i)),
            pl.BlockSpec((1, features), lambda i: (0, 0)),
        ],
        out_specs=block,
        out_shape=jax.ShapeDtypeStruct((count, features), BF16),
        compiler_params=params(),
        cost_estimate=pl.CostEstimate(flops=12_000_000_000, bytes_accessed=10_000_000, transcendentals=0),
        name="norm_backward",
    )(in_hbm(sent), in_hbm(other), in_hbm(frames), in_hbm(arrived), gain)


def pair_product(left, left_peer, right, right_peer, groups, first, buffer=None):
    rows, count = left.shape
    made, _, width = right.shape
    spec = pl.BlockSpec((None, count, width), lambda i: (i, 0, 0))
    whole = pl.BlockSpec((rows, count), lambda i: (0, 0))
    return pl.pallas_call(
        pair_kernel,
        grid=(made,),
        in_specs=[whole, whole, spec, spec] + ([] if buffer is None else [hbm()]),
        out_specs=pl.BlockSpec((rows, width), lambda i: (0, first + i)),
        out_shape=pltpu.HBM((rows, groups * width), BF16),
        input_output_aliases={} if buffer is None else {4: 0},
        compiler_params=params(),
        name="weight_gradient",
    )(left, left_peer, right, right_peer, *([] if buffer is None else [in_hbm(buffer)]))


def ring_shares(value, axis):
    return [value] + [lax.ppermute(value, axis, [(i, (i + by) % 4) for i in range(4)]) for by in (1, 2, 3)]


def ring_sum(shares):
    own, first, second, third = [share.astype(F32) for share in shares]
    return (own + second) + (first + third)


def finish_rows(summed, xl):
    own = lax.dynamic_index_in_dim(summed, xl, 0, keepdims=False)
    other = lax.dynamic_index_in_dim(summed, 1 - xl, 0, keepdims=False)
    return own + swap(other, "xl")


def body(frames, returned, norm_gain, weight_in, kernel, weight_out, block_utt, block_fill):
    count = frames.shape[0]
    width = weight_in.shape[2]
    features = frames.shape[1]
    blocks = count // BLOCK
    core, xl = lax.axis_index("core"), lax.axis_index("xl")
    first_block = lax.axis_index(FRAMES) * blocks
    chunks, frames = lax.optimization_barrier((frame_chunks(returned.T, 4), frames))
    frames_before, frames_after = halos(frames)
    arrived = lax.all_to_all(chunks, "section", 0, 0).reshape(features, count)

    edge = jnp.full((1,), -1, jnp.int32)
    near_utt = lax.dynamic_slice(jnp.concatenate([edge, block_utt, edge]), (first_block,), (blocks + 2,))
    near_fill = lax.dynamic_slice(jnp.concatenate([edge, block_fill, edge]), (first_block,), (blocks + 2,))
    same = (near_utt[1:] == near_utt[:-1]).astype(jnp.int32)
    fill = near_fill[1:-1]
    valid = (jnp.arange(BLOCK, dtype=jnp.int32)[None, :] < near_fill[:, None]).reshape(-1)
    valid = valid[BLOCK - HALO : BLOCK + count + HALO]

    normed_ext, normed_t = normalised(frames, frames_before, frames_after, norm_gain)
    value_proj = jnp.dot(normed_ext, weight_in[0], preferred_element_type=F32)
    gate_proj = jnp.dot(normed_ext, weight_in[1], preferred_element_type=F32)
    gate_sigmoid = jax.nn.sigmoid(gate_proj)
    units = jnp.where(valid[:, None], value_proj * gate_sigmoid, 0.0).astype(BF16)
    activated, slope = convolved(same, fill, units, kernel, count)
    activated_peer = swap(activated, "core")

    normed_own, normed_other = halves(core, normed_t)
    normed_peer = swap(normed_other, "core")

    arrived, normed_own, normed_other = lax.optimization_barrier((arrived, normed_own, normed_other))
    grad_activated = lax.dot_general(
        arrived, weight_out, (((0,), (1,)), ((), ())), preferred_element_type=F32
    )
    grad_conv = grad_activated * slope
    conv_before, conv_after = halos(grad_conv)
    rows_own, rows_other = halves(core, arrived)
    rows_peer = swap(rows_other, "core")
    parts = pair_product(rows_own, rows_peer, activated[None], activated_peer[None], 3, 0)

    ready, parts = lax.optimization_barrier((grad_conv, parts))
    late = projected_back(
        same, fill, ready, conv_before, conv_after, kernel, value_proj, gate_sigmoid
    )
    late_peer = swap(late, "core")
    contract = (((1,), (1,)), ((), ()))
    sent = lax.dot_general(late[0], weight_in[0], contract, preferred_element_type=F32)
    sent = sent + lax.dot_general(late[1], weight_in[1], contract, preferred_element_type=F32)
    sent = sent.astype(BF16)
    other = swap(sent, "tensor")
    late, sent = lax.optimization_barrier((late, sent))
    parts = pair_product(normed_own, normed_peer, late, late_peer, 3, 1, parts)
    got = lax.all_to_all(parts.reshape(16, 40, 3 * width), PLANE, 0, 0)

    ready, sent_again, _ = lax.optimization_barrier((grad_conv, sent, parts))
    taps_part = tap_sums(same, units, ready)
    gain_part = sent_again.astype(F32) * normed_ext[HALO : HALO + count].astype(F32)
    gain_part = jnp.sum(gain_part, axis=0) / norm_gain
    small = jnp.concatenate([taps_part, gain_part.reshape(2, width)], axis=0)
    small = small + swap(small, "core")
    gain = small[32:]
    corner = lax.ppermute(gain, ("xl", "tensor"), [(0, 3), (1, 2), (2, 1), (3, 0)])
    across = swap(small, "xl"), swap(gain, "tensor"), corner
    small, across, other = lax.optimization_barrier((small, across, other))
    gain = (small[32:] + across[1]) + (across[0][32:] + across[2])
    small = jnp.concatenate([small[:32] + across[0][:32], gain], axis=0)
    shares = ring_shares(small.astype(BF16), "y")
    grad_frames = norm_back(sent, other, frames, arrived, norm_gain.reshape(1, features))
    got, grad_frames = lax.optimization_barrier((got, grad_frames))
    total = jnp.sum(got.astype(F32), axis=0)
    total, shares = lax.optimization_barrier((total, shares))
    summed = finish_rows(total.reshape(2, 20, 3 * width), xl)
    small = ring_sum(ring_shares(ring_sum(shares).astype(BF16), "section"))
    grad_kernel = small[:TAPS]
    grad_gain = small[32:].reshape(features)
    grad_out = summed[:, :width].T
    grad_in = jnp.stack([summed[:, width : 2 * width], summed[:, 2 * width :]])
    return (grad_frames, grad_in, grad_out, grad_kernel, grad_gain)


def solution(mesh):
    split = Mesh(
        np.asarray(mesh.devices).reshape(2, 4, 2, 2, 4), ("xl", "y", "core", "tensor", "section")
    )
    outer = ("xl", "y", "core")
    in_specs = (
        P(FRAMES, None),
        P(outer, "section"),
        P(),
        P(None, None, "tensor"),
        P(None, "tensor"),
        P("tensor", None),
        P(),
        P(),
    )
    out_specs = (
        P(FRAMES, None),
        P(None, FRAMES, "tensor"),
        P("tensor", FRAMES),
        P(None, "tensor"),
        P(),
    )
    return jax.shard_map(body, mesh=split, in_specs=in_specs, out_specs=out_specs, check_vma=False)
```

```python
import functools

import jax
import jax.numpy as jnp
import numpy as np
from jax import lax
from jax.experimental import pallas as pl
from jax.experimental.pallas import tpu as pltpu
from jax.sharding import Mesh
from jax.sharding import PartitionSpec as P

BLOCK = 128
HALO = 16
TAPS = 31
LANES = 128
EPSILON = 1e-05
BF16 = jnp.bfloat16
F32 = jnp.float32

FRAMES = ("xl", "y", "core", "section")
PLANE = ("y", "section")
MIB = 1024 * 1024


def params(mib=16):
    return pltpu.CompilerParams(vmem_limit_bytes=mib * MIB)


def duration(us):
    return pl.CostEstimate(flops=round(us * 1.15e9), bytes_accessed=0, transcendentals=0)


def in_hbm(array):
    return pltpu.with_memory_space_constraint(array, pltpu.HBM)


def swap(value, axis):
    return lax.ppermute(value, axis, [(0, 1), (1, 0)])


def halos(shard):
    peers = lax.axis_size(FRAMES)
    odd = lax.axis_index(FRAMES) % 2 == 1
    first, last = shard[:HALO], shard[shard.shape[0] - HALO :]
    pairs = [(i, i ^ 1) for i in range(peers)]
    across = [(i, i + 1) for i in range(1, peers - 1, 2)]
    across = across + [(j, i) for i, j in across]
    inner = lax.ppermute(jnp.where(odd, first, last), FRAMES, pairs)
    outer = lax.ppermute(jnp.where(odd, last, first), FRAMES, across)
    return inner, outer


def fill_windows(win, main, inner, outer, same):
    odd = same[win.shape[0] + 1] == 1
    before = jnp.where(odd, inner[...], outer[...])
    after = jnp.where(odd, outer[...], inner[...])
    blocks = win.shape[0]
    for b in range(blocks):
        lo, hi = b * BLOCK, (b + 1) * BLOCK
        prior = before if b == 0 else main[lo - HALO : lo, :]
        later = after if b == blocks - 1 else main[hi : hi + HALO, :]
        win[b, HALO : HALO + BLOCK, :] = main[lo:hi, :].astype(F32)
        win[b, :HALO, :] = jnp.where(same[b] == 1, prior.astype(F32), 0.0)
        win[b, HALO + BLOCK :, :] = jnp.where(same[b + 1] == 1, later.astype(F32), 0.0)


def fill_extended(win, rows, same):
    for b in range(win.shape[0]):
        lo = b * BLOCK
        hi = lo + HALO + BLOCK
        win[b, HALO : HALO + BLOCK, :] = rows[lo + HALO : hi, :].astype(F32)
        win[b, :HALO, :] = jnp.where(same[b] == 1, rows[lo : lo + HALO, :].astype(F32), 0.0)
        win[b, HALO + BLOCK :, :] = jnp.where(same[b + 1] == 1, rows[hi : hi + HALO, :].astype(F32), 0.0)


def shifted(win, b, shift):
    first = 1 if shift == 0 else 0
    return [(8 * a + shift - 1, 8 * a) for a in range(first, 4)], win[b, pl.ds(shift, BLOCK + 24), :]


def convolve(win, b, taps, flip):
    total = jnp.zeros((BLOCK, LANES), F32)
    for shift in range(8):
        steps, rows = shifted(win, b, shift)
        for k, at in steps:
            row = TAPS - 1 - k if flip else k
            total = total + taps[row : row + 1, :] * rows[at : at + BLOCK]
    return total


def valid_rows(fill, b):
    return lax.broadcasted_iota(jnp.int32, (BLOCK, LANES), 0) < fill[b]


def forward_kernel(same, fill, units, taps, activated, slope, win):
    fill_extended(win, units, same)

    def step(b, carry):
        conv = convolve(win, b, taps, False)
        q = jax.nn.sigmoid(conv)
        valid = valid_rows(fill, b)
        rows = pl.ds(pl.multiple_of(b * BLOCK, BLOCK), BLOCK)
        activated[rows, :] = jnp.where(valid, conv * q, 0.0).astype(BF16)
        slope[rows, :] = jnp.where(valid, q + conv * q * (1.0 - q), 0.0)
        return carry

    lax.fori_loop(0, win.shape[0], step, 0)


def taps_kernel(same, units, grad_conv, out, win, sums):
    fill_extended(win, units, same)
    sums[...] = jnp.zeros_like(sums)

    def step(b, carry):
        grad = grad_conv[pl.ds(pl.multiple_of(b * BLOCK, BLOCK), BLOCK), :]
        for shift in range(8):
            steps, rows = shifted(win, b, shift)
            for k, at in steps:
                terms = (rows[at : at + BLOCK] * grad).reshape(BLOCK // 8, 8, LANES)
                sums[k] += jnp.sum(terms, axis=0)
        return carry

    lax.fori_loop(0, win.shape[0], step, 0)
    out[...] = jnp.sum(sums[...], axis=1)


def backward_kernel(same, fill, grad_conv, inner, outer, taps, value, gate, out, win):
    fill_windows(win, grad_conv, inner, outer, same)

    def step(b, carry):
        grad_units = jnp.where(valid_rows(fill, b), convolve(win, b, taps, True), 0.0)
        rows = pl.ds(pl.multiple_of(b * BLOCK, BLOCK), BLOCK)
        inner = pl.ds(pl.multiple_of(b * BLOCK + HALO, HALO), BLOCK)
        s = gate[inner, :]
        grad_value = grad_units * s
        out[0, rows, :] = grad_value.astype(BF16)
        out[1, rows, :] = (grad_value * value[inner, :] * (1.0 - s)).astype(BF16)
        return carry

    lax.fori_loop(0, win.shape[0], step, 0)


def norm_kernel(place, frames, inner, outer, gain, out, out_t):
    def rows(block):
        x = block.astype(F32)
        center = x - jnp.mean(x, axis=1, keepdims=True)
        inv = lax.rsqrt(jnp.mean(center * center, axis=1, keepdims=True) + EPSILON)
        return (center * inv * gain[...]).astype(BF16)

    i = pl.program_id(0)
    normed = rows(frames[...])
    out[pl.ds(pl.multiple_of(HALO + i * BLOCK, HALO), BLOCK), :] = normed
    out_t[...] = normed.T

    @pl.when(i == 0)
    def _():
        odd = place[2] % 2 == 1
        out[:HALO, :] = rows(jnp.where(odd, inner[...].astype(F32), outer[...].astype(F32)))
        out[out.shape[0] - HALO :, :] = rows(jnp.where(odd, outer[...].astype(F32), inner[...].astype(F32)))


def chunks_kernel(rows, out, held, sems):
    count = held.shape[2]
    parts = range(held.shape[0])
    loads = [pltpu.make_async_copy(rows.at[:, pl.ds(i * count, count)], held.at[i], sems.at[0, i]) for i in parts]
    stores = [pltpu.make_async_copy(held.at[i], out.at[i], sems.at[1, i]) for i in parts]
    for load in loads:
        load.start()
    for load, store in zip(loads, stores):
        load.wait()
        store.start()
    for store in stores:
        store.wait()


def halves_kernel(core, rows, order, own, other, held, sem):
    copy = pltpu.make_async_copy(held, other, sem)
    for half, out in ((1 - core[0], held), (core[0], own)):
        for y in range(4):
            first = pl.multiple_of(y * 160 + half * 80, 16)
            second = pl.multiple_of((4 + y) * 160 + half * 80, 16)
            both = jnp.concatenate([rows[pl.ds(first, 80), :], rows[pl.ds(second, 80), :]], axis=0)
            moved = jnp.dot(order[...], both, preferred_element_type=F32)
            out[y * 160 : (y + 1) * 160, :] = moved.astype(BF16)
        if out is held:
            copy.start()
    copy.wait()


def final_kernel(sent, other, frames, arrived, gain, out):
    x = frames[...].astype(F32)
    center = x - jnp.mean(x, axis=1, keepdims=True)
    inv = lax.rsqrt(jnp.mean(center * center, axis=1, keepdims=True) + EPSILON)
    unit = center * inv
    e = (sent[...].astype(F32) + other[...].astype(F32)) * gain[...]
    back = e - jnp.mean(e, axis=1, keepdims=True) - unit * jnp.mean(e * unit, axis=1, keepdims=True)
    out[...] = (arrived[...].astype(F32).T + inv * back).astype(BF16)


def pair_kernel(left, left_peer, right, right_peer, *buffers):
    out = buffers[-1]
    total = jnp.dot(left[...], right[...], preferred_element_type=F32)
    total = total + jnp.dot(left_peer[...], right_peer[...], preferred_element_type=F32)
    out[...] = total.astype(BF16)


def hbm():
    return pl.BlockSpec(memory_space=pltpu.HBM)


def smem():
    return pl.BlockSpec(memory_space=pltpu.SMEM)


def lanes(rows):
    return pl.BlockSpec((rows, LANES), lambda c: (0, c))


def convolved(same, fill, units, taps, count):
    width = units.shape[1]
    return pl.pallas_call(
        forward_kernel,
        grid=(width // LANES,),
        in_specs=[smem(), smem(), lanes(units.shape[0]), lanes(TAPS)],
        out_specs=[lanes(count), lanes(count)],
        out_shape=[
            jax.ShapeDtypeStruct((count, width), BF16),
            pltpu.HBM((count, width), F32),
        ],
        scratch_shapes=[pltpu.VMEM((count // BLOCK, BLOCK + 2 * HALO, LANES), F32)],
        compiler_params=params(),
        cost_estimate=duration(5),
        name="conv_forward",
    )(same, fill, units, taps)


def tap_sums(same, units, grad_conv):
    count, width = grad_conv.shape
    return pl.pallas_call(
        taps_kernel,
        grid=(width // LANES,),
        in_specs=[smem(), lanes(units.shape[0]), lanes(count)],
        out_specs=lanes(32),
        out_shape=jax.ShapeDtypeStruct((32, width), F32),
        scratch_shapes=[
            pltpu.VMEM((count // BLOCK, BLOCK + 2 * HALO, LANES), F32),
            pltpu.VMEM((32, 8, LANES), F32),
        ],
        compiler_params=params(),
        cost_estimate=duration(4),
        name="tap_gradients",
    )(same, units, grad_conv)


def projected_back(same, fill, grad_conv, before, after, taps, value, gate):
    count, width = grad_conv.shape
    return pl.pallas_call(
        backward_kernel,
        grid=(width // LANES,),
        in_specs=[
            smem(),
            smem(),
            lanes(count),
            lanes(HALO),
            lanes(HALO),
            lanes(TAPS),
            lanes(value.shape[0]),
            lanes(value.shape[0]),
        ],
        out_specs=pl.BlockSpec((2, count, LANES), lambda c: (0, 0, c)),
        out_shape=jax.ShapeDtypeStruct((2, count, width), BF16),
        scratch_shapes=[pltpu.VMEM((count // BLOCK, BLOCK + 2 * HALO, LANES), F32)],
        compiler_params=params(),
        cost_estimate=duration(5.6),
        name="conv_backward",
    )(same, fill, grad_conv, before, after, taps, in_hbm(value), in_hbm(gate))


def normalised(place, frames, inner, outer, gain):
    count, features = frames.shape
    edge = pl.BlockSpec((HALO, features), lambda i: (0, 0))
    return pl.pallas_call(
        norm_kernel,
        grid=(count // BLOCK,),
        in_specs=[
            smem(),
            pl.BlockSpec((BLOCK, features), lambda i: (i, 0)),
            edge,
            edge,
            pl.BlockSpec((1, features), lambda i: (0, 0)),
        ],
        out_specs=[
            pl.BlockSpec((count + 2 * HALO, features), lambda i: (0, 0)),
            pl.BlockSpec((features, BLOCK), lambda i: (0, i)),
        ],
        out_shape=[
            jax.ShapeDtypeStruct((count + 2 * HALO, features), BF16),
            jax.ShapeDtypeStruct((features, count), BF16),
        ],
        compiler_params=params(),
        cost_estimate=duration(3.5),
        name="layer_norm",
    )(place, in_hbm(frames), inner, outer, gain.reshape(1, features))


def frame_chunks(rows, parts):
    features, total = rows.shape
    shape = (parts, features, total // parts)
    return pl.pallas_call(
        chunks_kernel,
        in_specs=[hbm()],
        out_specs=hbm(),
        out_shape=pltpu.HBM(shape, rows.dtype),
        scratch_shapes=[pltpu.VMEM(shape, rows.dtype), pltpu.SemaphoreType.DMA((2, parts))],
        compiler_params=params(),
        cost_estimate=duration(2),
        name="frame_chunks",
    )(in_hbm(rows))


def halves(core, rows, keep=False):
    features, count = rows.shape
    order = np.zeros((160, 160), np.float32)
    for z in range(4):
        for x in range(2):
            for r in range(20):
                order[(z * 2 + x) * 20 + r, x * 80 + z * 20 + r] = 1.0
    vmem = pl.BlockSpec(memory_space=pltpu.VMEM)
    half = jax.ShapeDtypeStruct((features // 2, count), BF16)
    return pl.pallas_call(
        halves_kernel,
        in_specs=[smem(), vmem, vmem],
        out_specs=[vmem, hbm()],
        out_shape=[half if keep else pltpu.HBM(half.shape, BF16), pltpu.HBM(half.shape, BF16)],
        scratch_shapes=[pltpu.VMEM(half.shape, BF16), pltpu.SemaphoreType.DMA],
        compiler_params=params(),
        cost_estimate=duration(1.2),
        name="core_halves",
    )(core.reshape(1), rows, jnp.asarray(order, BF16))


def norm_back(sent, other, frames, arrived, gain):
    count, features = frames.shape
    block = pl.BlockSpec((BLOCK, features), lambda i: (i, 0))
    return pl.pallas_call(
        final_kernel,
        grid=(count // BLOCK,),
        in_specs=[
            block,
            block,
            block,
            pl.BlockSpec((features, BLOCK), lambda i: (0, i)),
            pl.BlockSpec((1, features), lambda i: (0, 0)),
        ],
        out_specs=block,
        out_shape=jax.ShapeDtypeStruct((count, features), BF16),
        compiler_params=params(),
        cost_estimate=duration(10.4),
        name="norm_backward",
    )(in_hbm(sent), in_hbm(other), in_hbm(frames), in_hbm(arrived), gain)


def pair_product(left, left_peer, right, right_peer, groups, first, buffer=None):
    rows, count = left.shape
    made, _, width = right.shape
    spec = pl.BlockSpec((None, count, width), lambda i: (i, 0, 0))
    whole = pl.BlockSpec((rows, count), lambda i: (0, 0))
    return pl.pallas_call(
        pair_kernel,
        grid=(made,),
        in_specs=[whole, whole, spec, spec] + ([] if buffer is None else [hbm()]),
        out_specs=pl.BlockSpec((rows, width), lambda i: (0, first + i)),
        out_shape=pltpu.HBM((rows, groups * width), BF16),
        input_output_aliases={} if buffer is None else {4: 0},
        compiler_params=params(),
        cost_estimate=duration(3.4),
        name="weight_gradient",
    )(left, left_peer, right, right_peer, *([] if buffer is None else [in_hbm(buffer)]))


def shares_of(value, axis):
    return [value] + [lax.ppermute(value, axis, [(i, i ^ k) for i in range(4)]) for k in (1, 2, 3)]


def sum_of(shares):
    own, first, second, third = [share.astype(F32) for share in shares]
    return (own + first) + (second + third)


def finish_rows(summed, xl):
    own = lax.dynamic_index_in_dim(summed, xl, 0, keepdims=False)
    other = lax.dynamic_index_in_dim(summed, 1 - xl, 0, keepdims=False)
    return own + swap(other, "xl")


def body(frames, returned, norm_gain, weight_in, kernel, weight_out, block_utt, block_fill):
    count = frames.shape[0]
    width = weight_in.shape[2]
    features = frames.shape[1]
    blocks = count // BLOCK
    core, xl = lax.axis_index("core"), lax.axis_index("xl")
    first_block = lax.axis_index(FRAMES) * blocks
    place = jnp.stack([core, lax.axis_index("y"), lax.axis_index("section")]).astype(jnp.int32)
    chunks, frames = lax.optimization_barrier((frame_chunks(returned.T, 4), frames))
    arrived = lax.all_to_all(chunks, "section", 0, 0).reshape(features, count)

    edge = jnp.full((1,), -1, jnp.int32)
    near_utt = lax.dynamic_slice(jnp.concatenate([edge, block_utt, edge]), (first_block,), (blocks + 2,))
    near_fill = lax.dynamic_slice(jnp.concatenate([edge, block_fill, edge]), (first_block,), (blocks + 2,))
    same = (near_utt[1:] == near_utt[:-1]).astype(jnp.int32)
    same = jnp.concatenate([same, lax.axis_index(FRAMES)[None].astype(jnp.int32) % 2])
    fill = near_fill[1:-1]
    valid = (jnp.arange(BLOCK, dtype=jnp.int32)[None, :] < near_fill[:, None]).reshape(-1)
    valid = valid[BLOCK - HALO : BLOCK + count + HALO]

    normed_ext, normed_t = normalised(place, frames, *halos(frames), norm_gain)
    value_proj = jnp.dot(normed_ext, weight_in[0], preferred_element_type=F32)
    gate_proj = jnp.dot(normed_ext, weight_in[1], preferred_element_type=F32)
    gate_sigmoid = jax.nn.sigmoid(gate_proj)
    units = jnp.where(valid[:, None], value_proj * gate_sigmoid, 0.0).astype(BF16)
    activated, slope = convolved(same, fill, units, kernel, count)
    activated_peer = swap(activated, "core")

    normed_own, normed_other = halves(core, normed_t)
    normed_peer = swap(normed_other, "core")

    arrived, normed_own, normed_other = lax.optimization_barrier((arrived, normed_own, normed_other))
    grad_activated = lax.dot_general(
        arrived, weight_out, (((0,), (1,)), ((), ())), preferred_element_type=F32
    )
    grad_conv = grad_activated * slope
    conv_inner, conv_outer = halos(grad_conv)
    arrived_rows, grad_conv = lax.optimization_barrier((arrived, grad_conv))
    rows_own, rows_other = halves(core, arrived_rows, keep=True)
    rows_peer = swap(rows_other, "core")
    parts = pair_product(rows_own, rows_peer, activated[None], activated_peer[None], 3, 0)

    ready, parts = lax.optimization_barrier((grad_conv, parts))
    late = projected_back(
        same, fill, ready, conv_inner, conv_outer, kernel, value_proj, gate_sigmoid
    )
    late_peer = swap(late, "core")
    contract = (((1,), (1,)), ((), ()))
    sent = lax.dot_general(late[0], weight_in[0], contract, preferred_element_type=F32)
    sent = sent + lax.dot_general(late[1], weight_in[1], contract, preferred_element_type=F32)
    sent = sent.astype(BF16)
    other = swap(sent, "tensor")
    late, sent = lax.optimization_barrier((late, sent))
    parts = pair_product(normed_own, normed_peer, late, late_peer, 3, 1, parts)
    got = lax.all_to_all(parts.reshape(16, 40, 3 * width), PLANE, 0, 0)

    ready, sent_again, _ = lax.optimization_barrier((grad_conv, sent, parts))
    taps_part = tap_sums(same, units, ready)
    gain_part = sent_again.astype(F32) * normed_ext[HALO : HALO + count].astype(F32)
    gain_part = jnp.sum(gain_part, axis=0) / norm_gain
    small = jnp.concatenate([taps_part, gain_part.reshape(2, width)], axis=0)
    small = small + swap(small, "core")
    gain = small[32:]
    corner = lax.ppermute(gain, ("xl", "tensor"), [(0, 3), (1, 2), (2, 1), (3, 0)])
    across = swap(small, "xl"), swap(gain, "tensor"), corner
    grad_frames = norm_back(sent, other, frames, arrived, norm_gain.reshape(1, features))
    small, across, grad_frames = lax.optimization_barrier((small, across, grad_frames))
    gain = (small[32:] + across[1]) + (across[0][32:] + across[2])
    small = jnp.concatenate([small[:32] + across[0][:32], gain], axis=0)
    shares = shares_of(small.astype(BF16), "y")
    got, grad_frames = lax.optimization_barrier((got, grad_frames))
    total = jnp.sum(got.astype(F32), axis=0)
    total, shares = lax.optimization_barrier((total, shares))
    summed = finish_rows(total.reshape(2, 20, 3 * width), xl)
    small = sum_of(shares_of(sum_of(shares).astype(BF16), "section"))
    grad_kernel = small[:TAPS]
    grad_gain = small[32:].reshape(features)
    grad_out = summed[:, :width].T
    grad_in = jnp.stack([summed[:, width : 2 * width], summed[:, 2 * width :]])
    return (grad_frames, grad_in, grad_out, grad_kernel, grad_gain)


def solution(mesh):
    split = Mesh(
        np.asarray(mesh.devices).reshape(2, 4, 2, 2, 4), ("xl", "y", "core", "tensor", "section")
    )
    outer = ("xl", "y", "core")
    in_specs = (
        P(FRAMES, None),
        P(outer, "section"),
        P(),
        P(None, None, "tensor"),
        P(None, "tensor"),
        P("tensor", None),
        P(),
        P(),
    )
    out_specs = (
        P(FRAMES, None),
        P(None, FRAMES, "tensor"),
        P("tensor", FRAMES),
        P(None, "tensor"),
        P(),
    )
    return jax.shard_map(body, mesh=split, in_specs=in_specs, out_specs=out_specs, check_vma=False)
```

```python
import functools

import jax
import jax.numpy as jnp
import numpy as np
from jax import lax
from jax.experimental import pallas as pl
from jax.experimental.pallas import tpu as pltpu
from jax.sharding import Mesh
from jax.sharding import PartitionSpec as P

BLOCK = 128
HALO = 16
TAPS = 31
LANES = 128
EPSILON = 1e-05
BF16 = jnp.bfloat16
F32 = jnp.float32

FRAMES = ("xl", "y", "core", "section")
PLANE = ("y", "section")
MIB = 1024 * 1024


def params(mib=16):
    return pltpu.CompilerParams(vmem_limit_bytes=mib * MIB)


def duration(us):
    return pl.CostEstimate(flops=round(us * 1.15e9), bytes_accessed=0, transcendentals=0)


def in_hbm(array):
    return pltpu.with_memory_space_constraint(array, pltpu.HBM)


def swap(value, axis):
    return lax.ppermute(value, axis, [(0, 1), (1, 0)])


def halos(shard):
    peers = lax.axis_size(FRAMES)
    odd = lax.axis_index(FRAMES) % 2 == 1
    first, last = shard[:HALO], shard[shard.shape[0] - HALO :]
    pairs = [(i, i ^ 1) for i in range(peers)]
    across = [(i, i + 1) for i in range(1, peers - 1, 2)]
    across = across + [(j, i) for i, j in across]
    inner = lax.ppermute(jnp.where(odd, first, last), FRAMES, pairs)
    outer = lax.ppermute(jnp.where(odd, last, first), FRAMES, across)
    return inner, outer


def each_lane_block(width, step):
    def block(c, carry):
        step(pl.ds(pl.multiple_of(c * LANES, LANES), LANES), c)
        return carry

    lax.fori_loop(0, width // LANES, block, 0)


def fill_windows(win, main, inner, outer, same, lane):
    odd = same[win.shape[0] + 1] == 1
    before = jnp.where(odd, inner[:, lane], outer[:, lane])
    after = jnp.where(odd, outer[:, lane], inner[:, lane])
    blocks = win.shape[0]
    for b in range(blocks):
        lo, hi = b * BLOCK, (b + 1) * BLOCK
        prior = before if b == 0 else main[lo - HALO : lo, lane]
        later = after if b == blocks - 1 else main[hi : hi + HALO, lane]
        win[b, HALO : HALO + BLOCK, :] = main[lo:hi, lane].astype(F32)
        win[b, :HALO, :] = jnp.where(same[b] == 1, prior.astype(F32), 0.0)
        win[b, HALO + BLOCK :, :] = jnp.where(same[b + 1] == 1, later.astype(F32), 0.0)


def fill_extended(win, rows, same, lane):
    for b in range(win.shape[0]):
        lo = b * BLOCK
        hi = lo + HALO + BLOCK
        win[b, HALO : HALO + BLOCK, :] = rows[lo + HALO : hi, lane].astype(F32)
        win[b, :HALO, :] = jnp.where(same[b] == 1, rows[lo : lo + HALO, lane].astype(F32), 0.0)
        win[b, HALO + BLOCK :, :] = jnp.where(same[b + 1] == 1, rows[hi : hi + HALO, lane].astype(F32), 0.0)


def shifted(win, b, shift):
    first = 1 if shift == 0 else 0
    return [(8 * a + shift - 1, 8 * a) for a in range(first, 4)], win[b, pl.ds(shift, BLOCK + 24), :]


def convolve(win, b, taps, lane, flip):
    total = jnp.zeros((BLOCK, LANES), F32)
    for shift in range(8):
        steps, rows = shifted(win, b, shift)
        for k, at in steps:
            row = TAPS - 1 - k if flip else k
            total = total + taps[row : row + 1, lane] * rows[at : at + BLOCK]
    return total


def valid_rows(fill, b):
    return lax.broadcasted_iota(jnp.int32, (BLOCK, LANES), 0) < fill[b]


def forward_kernel(same, fill, units, taps, activated, slope, win, held_act, held_slope, sems):
    def stores(lane, c):
        return (
            pltpu.make_async_copy(held_act.at[:, lane], activated.at[:, lane], sems.at[0, c]),
            pltpu.make_async_copy(held_slope.at[:, lane], slope.at[:, lane], sems.at[1, c]),
        )

    def step(lane, c):
        fill_extended(win, units, same, lane)
        for b in range(win.shape[0]):
            conv = convolve(win, b, taps, lane, False)
            q = jax.nn.sigmoid(conv)
            valid = valid_rows(fill, b)
            rows = slice(b * BLOCK, (b + 1) * BLOCK)
            held_act[rows, lane] = jnp.where(valid, conv * q, 0.0).astype(BF16)
            held_slope[rows, lane] = jnp.where(valid, q + conv * q * (1.0 - q), 0.0)
        for copy in stores(lane, c):
            copy.start()

    each_lane_block(units.shape[1], step)
    for c in range(units.shape[1] // LANES):
        for copy in stores(pl.ds(c * LANES, LANES), c):
            copy.wait()


def taps_kernel(same, units, grad_conv, out, win, sums):
    def step(lane, c):
        fill_extended(win, units, same, lane)
        sums[...] = jnp.zeros_like(sums)
        for b in range(win.shape[0]):
            grad = grad_conv[b * BLOCK : (b + 1) * BLOCK, lane]
            for shift in range(8):
                steps, rows = shifted(win, b, shift)
                for k, at in steps:
                    terms = (rows[at : at + BLOCK] * grad).reshape(BLOCK // 8, 8, LANES)
                    sums[k] += jnp.sum(terms, axis=0)
        out[:, lane] = jnp.sum(sums[...], axis=1)

    each_lane_block(units.shape[1], step)


def backward_kernel(same, fill, grad_conv, inner, outer, taps, value, gate, out, win):
    def step(lane, c):
        fill_windows(win, grad_conv, inner, outer, same, lane)
        for b in range(win.shape[0]):
            grad_units = jnp.where(valid_rows(fill, b), convolve(win, b, taps, lane, True), 0.0)
            rows = slice(b * BLOCK, (b + 1) * BLOCK)
            own = slice(b * BLOCK + HALO, (b + 1) * BLOCK + HALO)
            s = gate[own, lane]
            grad_value = grad_units * s
            out[0, rows, lane] = grad_value.astype(BF16)
            out[1, rows, lane] = (grad_value * value[own, lane] * (1.0 - s)).astype(BF16)

    each_lane_block(grad_conv.shape[1], step)


def norm_kernel(place, frames, inner, outer, gain, out, out_t):
    def rows(block):
        x = block.astype(F32)
        center = x - jnp.mean(x, axis=1, keepdims=True)
        inv = lax.rsqrt(jnp.mean(center * center, axis=1, keepdims=True) + EPSILON)
        return (center * inv * gain[...]).astype(BF16)

    for first in range(0, frames.shape[0], BLOCK):
        normed = rows(frames[first : first + BLOCK, :])
        out[HALO + first : HALO + first + BLOCK, :] = normed
        out_t[:, first : first + BLOCK] = normed.T
    odd = place[2] % 2 == 1
    out[:HALO, :] = rows(jnp.where(odd, inner[...].astype(F32), outer[...].astype(F32)))
    out[out.shape[0] - HALO :, :] = rows(jnp.where(odd, outer[...].astype(F32), inner[...].astype(F32)))


def chunks_kernel(section, rows, *refs):
    outs, held, sems = refs[:4], refs[4], refs[5]
    count = held.shape[2]
    loads, stores = [], []
    for k, out in enumerate(outs):
        first = pl.multiple_of((section[0] ^ k) * count, count)
        loads.append(pltpu.make_async_copy(rows.at[:, pl.ds(first, count)], held.at[k], sems.at[0, k]))
        stores.append(pltpu.make_async_copy(held.at[k], out, sems.at[1, k]))
    for load in loads[1:] + loads[:1]:
        load.start()
    for k in (1, 2, 3, 0):
        loads[k].wait()
        stores[k].start()
    for store in stores:
        store.wait()


def gradient_kernel(section, own, first, second, third, weights, slope, arrived, out, sems):
    pieces = own, first, second, third
    rows = own.shape[0]
    copies = []
    for k, piece in enumerate(pieces):
        at = pl.multiple_of((section[0] ^ k) * rows, 64)
        copies.append(pltpu.make_async_copy(piece, arrived.at[pl.ds(at, rows), :], sems.at[k]))
    for copy in copies:
        copy.start()
    for copy in copies:
        copy.wait()
    grad = jnp.dot(weights[...], arrived[...], preferred_element_type=F32)
    out[...] = grad.T * slope[...]


def halves_kernel(core, rows, order, own, other, held, sem):
    copy = pltpu.make_async_copy(held, other, sem)
    for half, out in ((1 - core[0], held), (core[0], own)):
        for y in range(4):
            first = pl.multiple_of(y * 160 + half * 80, 16)
            second = pl.multiple_of((4 + y) * 160 + half * 80, 16)
            both = jnp.concatenate([rows[pl.ds(first, 80), :], rows[pl.ds(second, 80), :]], axis=0)
            moved = jnp.dot(order[...], both, preferred_element_type=F32)
            out[y * 160 : (y + 1) * 160, :] = moved.astype(BF16)
        if out is held:
            copy.start()
    copy.wait()


def final_kernel(sent, other, frames, arrived, gain, out):
    x = frames[...].astype(F32)
    center = x - jnp.mean(x, axis=1, keepdims=True)
    inv = lax.rsqrt(jnp.mean(center * center, axis=1, keepdims=True) + EPSILON)
    unit = center * inv
    e = (sent[...].astype(F32) + other[...].astype(F32)) * gain[...]
    back = e - jnp.mean(e, axis=1, keepdims=True) - unit * jnp.mean(e * unit, axis=1, keepdims=True)
    out[...] = (arrived[...].astype(F32).T + inv * back).astype(BF16)


def pair_kernel(left, left_peer, right, right_peer, *buffers):
    out = buffers[-1]
    total = jnp.dot(left[...], right[...], preferred_element_type=F32)
    total = total + jnp.dot(left_peer[...], right_peer[...], preferred_element_type=F32)
    out[...] = total.astype(BF16)


def hbm():
    return pl.BlockSpec(memory_space=pltpu.HBM)


def smem():
    return pl.BlockSpec(memory_space=pltpu.SMEM)


def vmem():
    return pl.BlockSpec(memory_space=pltpu.VMEM)


def windows(count):
    return pltpu.VMEM((count // BLOCK, BLOCK + 2 * HALO, LANES), F32)


def convolved(same, fill, units, taps, count):
    width = units.shape[1]
    return pl.pallas_call(
        forward_kernel,
        in_specs=[smem(), smem(), vmem(), vmem()],
        out_specs=[hbm(), hbm()],
        out_shape=[pltpu.HBM((count, width), BF16), pltpu.HBM((count, width), F32)],
        scratch_shapes=[
            windows(count),
            pltpu.VMEM((count, width), BF16),
            pltpu.VMEM((count, width), F32),
            pltpu.SemaphoreType.DMA((2, width // LANES)),
        ],
        compiler_params=params(),
        cost_estimate=duration(5),
        name="conv_forward",
    )(same, fill, units, taps)


def tap_sums(same, units, grad_conv):
    count, width = grad_conv.shape
    return pl.pallas_call(
        taps_kernel,
        in_specs=[smem(), vmem(), vmem()],
        out_specs=vmem(),
        out_shape=jax.ShapeDtypeStruct((32, width), F32),
        scratch_shapes=[windows(count), pltpu.VMEM((32, 8, LANES), F32)],
        compiler_params=params(),
        cost_estimate=duration(4),
        name="tap_gradients",
    )(same, units, grad_conv)


def projected_back(same, fill, grad_conv, inner, outer, taps, value, gate):
    count, width = grad_conv.shape
    return pl.pallas_call(
        backward_kernel,
        in_specs=[smem(), smem()] + [vmem()] * 6,
        out_specs=vmem(),
        out_shape=jax.ShapeDtypeStruct((2, count, width), BF16),
        scratch_shapes=[windows(count)],
        compiler_params=params(),
        cost_estimate=duration(5.6),
        name="conv_backward",
    )(same, fill, grad_conv, inner, outer, taps, value, gate)


def normalised(place, frames, inner, outer, gain):
    count, features = frames.shape
    return pl.pallas_call(
        norm_kernel,
        in_specs=[smem()] + [vmem()] * 4,
        out_specs=[vmem(), vmem()],
        out_shape=[
            jax.ShapeDtypeStruct((count + 2 * HALO, features), BF16),
            jax.ShapeDtypeStruct((features, count), BF16),
        ],
        compiler_params=params(),
        cost_estimate=duration(3.5),
        name="layer_norm",
    )(place, frames, inner, outer, gain.reshape(1, features))


def frame_chunks(section, rows):
    features, total = rows.shape
    count = total // 4
    return pl.pallas_call(
        chunks_kernel,
        in_specs=[smem(), hbm()],
        out_specs=[hbm()] * 4,
        out_shape=[pltpu.HBM((features, count), rows.dtype)] * 4,
        scratch_shapes=[pltpu.VMEM((4, features, count), rows.dtype), pltpu.SemaphoreType.DMA((2, 4))],
        compiler_params=params(),
        cost_estimate=duration(2),
        name="frame_chunks",
    )(section, in_hbm(rows))


def conv_gradient(section, pieces, weights, slope):
    features, count = 4 * pieces[0].shape[0], pieces[0].shape[1]
    return pl.pallas_call(
        gradient_kernel,
        in_specs=[smem()] + [hbm()] * 4 + [vmem()] * 2,
        out_specs=[vmem()] * 2,
        out_shape=[
            jax.ShapeDtypeStruct((features, count), BF16),
            jax.ShapeDtypeStruct((count, weights.shape[0]), F32),
        ],
        scratch_shapes=[pltpu.SemaphoreType.DMA((4,))],
        compiler_params=params(),
        cost_estimate=duration(3),
        name="conv_gradient",
    )(section, *[in_hbm(piece) for piece in pieces], weights, slope)


def halves(core, rows, keep=False):
    features, count = rows.shape
    order = np.zeros((160, 160), np.float32)
    for z in range(4):
        for x in range(2):
            for r in range(20):
                order[(z * 2 + x) * 20 + r, x * 80 + z * 20 + r] = 1.0
    half = jax.ShapeDtypeStruct((features // 2, count), BF16)
    return pl.pallas_call(
        halves_kernel,
        in_specs=[smem(), vmem(), vmem()],
        out_specs=[vmem(), hbm()],
        out_shape=[half if keep else pltpu.HBM(half.shape, BF16), pltpu.HBM(half.shape, BF16)],
        scratch_shapes=[pltpu.VMEM(half.shape, BF16), pltpu.SemaphoreType.DMA],
        compiler_params=params(),
        cost_estimate=duration(1.2),
        name="core_halves",
    )(core.reshape(1), rows, jnp.asarray(order, BF16))


def norm_back(sent, other, frames, arrived, gain):
    count, features = frames.shape
    block = pl.BlockSpec((BLOCK, features), lambda i: (i, 0))
    return pl.pallas_call(
        final_kernel,
        grid=(count // BLOCK,),
        in_specs=[
            block,
            block,
            block,
            pl.BlockSpec((features, BLOCK), lambda i: (0, i)),
            pl.BlockSpec((1, features), lambda i: (0, 0)),
        ],
        out_specs=block,
        out_shape=jax.ShapeDtypeStruct((count, features), BF16),
        compiler_params=params(),
        cost_estimate=duration(10.4),
        name="norm_backward",
    )(in_hbm(sent), in_hbm(other), in_hbm(frames), in_hbm(arrived), gain)


def pair_product(left, left_peer, right, right_peer, groups, first, buffer=None):
    rows, count = left.shape
    made, _, width = right.shape
    spec = pl.BlockSpec((None, count, width), lambda i: (i, 0, 0))
    whole = pl.BlockSpec((rows, count), lambda i: (0, 0))
    return pl.pallas_call(
        pair_kernel,
        grid=(made,),
        in_specs=[whole, whole, spec, spec] + ([] if buffer is None else [hbm()]),
        out_specs=pl.BlockSpec((rows, width), lambda i: (0, first + i)),
        out_shape=pltpu.HBM((rows, groups * width), BF16),
        input_output_aliases={} if buffer is None else {4: 0},
        compiler_params=params(),
        cost_estimate=duration(3.4),
        name="weight_gradient",
    )(left, left_peer, right, right_peer, *([] if buffer is None else [in_hbm(buffer)]))


def shares_of(value, axis):
    return [value] + [lax.ppermute(value, axis, [(i, i ^ k) for i in range(4)]) for k in (1, 2, 3)]


def sum_of(shares):
    own, first, second, third = [share.astype(F32) for share in shares]
    return (own + first) + (second + third)


def finish_rows(summed, xl):
    own = lax.dynamic_index_in_dim(summed, xl, 0, keepdims=False)
    other = lax.dynamic_index_in_dim(summed, 1 - xl, 0, keepdims=False)
    return own + swap(other, "xl")


def body(frames, returned, norm_gain, weight_in, kernel, weight_out, block_utt, block_fill):
    count = frames.shape[0]
    width = weight_in.shape[2]
    features = frames.shape[1]
    blocks = count // BLOCK
    core, xl = lax.axis_index("core"), lax.axis_index("xl")
    first_block = lax.axis_index(FRAMES) * blocks
    place = jnp.stack([core, lax.axis_index("y"), lax.axis_index("section")]).astype(jnp.int32)
    section = lax.axis_index("section").reshape(1)
    *chunks, frames = lax.optimization_barrier((*frame_chunks(section, returned.T), frames))
    for k in (1, 3, 2):
        chunks[k] = lax.ppermute(chunks[k], "section", [(i, i ^ k) for i in range(4)])

    edge = jnp.full((1,), -1, jnp.int32)
    near_utt = lax.dynamic_slice(jnp.concatenate([edge, block_utt, edge]), (first_block,), (blocks + 2,))
    near_fill = lax.dynamic_slice(jnp.concatenate([edge, block_fill, edge]), (first_block,), (blocks + 2,))
    same = (near_utt[1:] == near_utt[:-1]).astype(jnp.int32)
    same = jnp.concatenate([same, lax.axis_index(FRAMES)[None].astype(jnp.int32) % 2])
    fill = near_fill[1:-1]
    valid = (jnp.arange(BLOCK, dtype=jnp.int32)[None, :] < near_fill[:, None]).reshape(-1)
    valid = valid[BLOCK - HALO : BLOCK + count + HALO]

    normed_ext, normed_t = normalised(place, frames, *halos(frames), norm_gain)
    value_proj = jnp.dot(normed_ext, weight_in[0], preferred_element_type=F32)
    gate_proj = jnp.dot(normed_ext, weight_in[1], preferred_element_type=F32)
    gate_sigmoid = jax.nn.sigmoid(gate_proj)
    units = jnp.where(valid[:, None], value_proj * gate_sigmoid, 0.0).astype(BF16)
    activated, slope = convolved(same, fill, units, kernel, count)
    activated_peer = swap(activated, "core")

    normed_own, normed_other = halves(core, normed_t)
    normed_peer = swap(normed_other, "core")

    arrived, grad_conv = conv_gradient(section, chunks, weight_out, slope)
    normed_own, normed_other, grad_conv = lax.optimization_barrier((normed_own, normed_other, grad_conv))
    conv_inner, conv_outer = halos(grad_conv)
    arrived_rows, grad_conv = lax.optimization_barrier((arrived, grad_conv))
    rows_own, rows_other = halves(core, arrived_rows, keep=True)
    rows_peer = swap(rows_other, "core")
    parts = pair_product(rows_own, rows_peer, activated[None], activated_peer[None], 3, 0)

    ready, parts = lax.optimization_barrier((grad_conv, parts))
    late = projected_back(
        same, fill, ready, conv_inner, conv_outer, kernel, value_proj, gate_sigmoid
    )
    late_peer = swap(late, "core")
    contract = (((1,), (1,)), ((), ()))
    sent = lax.dot_general(late[0], weight_in[0], contract, preferred_element_type=F32)
    sent = sent + lax.dot_general(late[1], weight_in[1], contract, preferred_element_type=F32)
    sent = sent.astype(BF16)
    other = swap(sent, "tensor")
    late, sent = lax.optimization_barrier((late, sent))
    parts = pair_product(normed_own, normed_peer, late, late_peer, 3, 1, parts)
    got = lax.all_to_all(parts.reshape(16, 40, 3 * width), PLANE, 0, 0)

    ready, sent_again, _ = lax.optimization_barrier((grad_conv, sent, parts))
    taps_part = tap_sums(same, units, ready)
    gain_part = sent_again.astype(F32) * normed_ext[HALO : HALO + count].astype(F32)
    gain_part = jnp.sum(gain_part, axis=0) / norm_gain
    small = jnp.concatenate([taps_part, gain_part.reshape(2, width)], axis=0)
    small = small + swap(small, "core")
    gain = small[32:]
    corner = lax.ppermute(gain, ("xl", "tensor"), [(0, 3), (1, 2), (2, 1), (3, 0)])
    across = swap(small, "xl"), swap(gain, "tensor"), corner
    grad_frames = norm_back(sent, other, frames, arrived, norm_gain.reshape(1, features))
    small, across, grad_frames = lax.optimization_barrier((small, across, grad_frames))
    gain = (small[32:] + across[1]) + (across[0][32:] + across[2])
    small = jnp.concatenate([small[:32] + across[0][:32], gain], axis=0)
    shares = shares_of(small.astype(BF16), "y")
    got, grad_frames = lax.optimization_barrier((got, grad_frames))
    total = jnp.sum(got.astype(F32), axis=0)
    total, shares = lax.optimization_barrier((total, shares))
    summed = finish_rows(total.reshape(2, 20, 3 * width), xl)
    small = sum_of(shares_of(sum_of(shares).astype(BF16), "section"))
    grad_kernel = small[:TAPS]
    grad_gain = small[32:].reshape(features)
    grad_out = summed[:, :width].T
    grad_in = jnp.stack([summed[:, width : 2 * width], summed[:, 2 * width :]])
    return (grad_frames, grad_in, grad_out, grad_kernel, grad_gain)


def solution(mesh):
    split = Mesh(
        np.asarray(mesh.devices).reshape(2, 4, 2, 2, 4), ("xl", "y", "core", "tensor", "section")
    )
    outer = ("xl", "y", "core")
    in_specs = (
        P(FRAMES, None),
        P(outer, "section"),
        P(),
        P(None, None, "tensor"),
        P(None, "tensor"),
        P("tensor", None),
        P(),
        P(),
    )
    out_specs = (
        P(FRAMES, None),
        P(None, FRAMES, "tensor"),
        P("tensor", FRAMES),
        P(None, "tensor"),
        P(),
    )
    return jax.shard_map(body, mesh=split, in_specs=in_specs, out_specs=out_specs, check_vma=False)
```

```python
import functools

import jax
import jax.numpy as jnp
import numpy as np
from jax import lax
from jax.experimental import pallas as pl
from jax.experimental.pallas import tpu as pltpu
from jax.sharding import Mesh
from jax.sharding import PartitionSpec as P

BLOCK = 128
HALO = 16
TAPS = 31
LANES = 128
EPSILON = 1e-05
BF16 = jnp.bfloat16
F32 = jnp.float32

FRAMES = ("xl", "y", "core", "section")
PLANE = ("y", "section")
MIB = 1024 * 1024


def params(mib=16):
    return pltpu.CompilerParams(vmem_limit_bytes=mib * MIB)


def duration(us):
    return pl.CostEstimate(flops=round(us * 1.15e9), bytes_accessed=0, transcendentals=0)


def in_hbm(array):
    return pltpu.with_memory_space_constraint(array, pltpu.HBM)


def swap(value, axis):
    return lax.ppermute(value, axis, [(0, 1), (1, 0)])


def halos(shard):
    peers = lax.axis_size(FRAMES)
    odd = lax.axis_index(FRAMES) % 2 == 1
    first, last = shard[:HALO], shard[shard.shape[0] - HALO :]
    pairs = [(i, i ^ 1) for i in range(peers)]
    across = [(i, i + 1) for i in range(1, peers - 1, 2)]
    across = across + [(j, i) for i, j in across]
    inner = lax.ppermute(jnp.where(odd, first, last), FRAMES, pairs)
    outer = lax.ppermute(jnp.where(odd, last, first), FRAMES, across)
    return inner, outer


def each_lane_block(width, step):
    def block(c, carry):
        step(pl.ds(pl.multiple_of(c * LANES, LANES), LANES), c)
        return carry

    lax.fori_loop(0, width // LANES, block, 0)


def fill_windows(win, main, inner, outer, same, lane):
    odd = same[win.shape[0] + 1] == 1
    before = jnp.where(odd, inner[:, lane], outer[:, lane])
    after = jnp.where(odd, outer[:, lane], inner[:, lane])
    blocks = win.shape[0]
    for b in range(blocks):
        lo, hi = b * BLOCK, (b + 1) * BLOCK
        prior = before if b == 0 else main[lo - HALO : lo, lane]
        later = after if b == blocks - 1 else main[hi : hi + HALO, lane]
        win[b, HALO : HALO + BLOCK, :] = main[lo:hi, lane].astype(F32)
        win[b, :HALO, :] = jnp.where(same[b] == 1, prior.astype(F32), 0.0)
        win[b, HALO + BLOCK :, :] = jnp.where(same[b + 1] == 1, later.astype(F32), 0.0)


def fill_extended(win, rows, same, lane):
    for b in range(win.shape[0]):
        lo = b * BLOCK
        hi = lo + HALO + BLOCK
        win[b, HALO : HALO + BLOCK, :] = rows[lo + HALO : hi, lane].astype(F32)
        win[b, :HALO, :] = jnp.where(same[b] == 1, rows[lo : lo + HALO, lane].astype(F32), 0.0)
        win[b, HALO + BLOCK :, :] = jnp.where(same[b + 1] == 1, rows[hi : hi + HALO, lane].astype(F32), 0.0)


def shifted(win, b, shift):
    first = 1 if shift == 0 else 0
    return [(8 * a + shift - 1, 8 * a) for a in range(first, 4)], win[b, pl.ds(shift, BLOCK + 24), :]


def convolve(win, b, taps, lane, flip):
    total = jnp.zeros((BLOCK, LANES), F32)
    for shift in range(8):
        steps, rows = shifted(win, b, shift)
        for k, at in steps:
            row = TAPS - 1 - k if flip else k
            total = total + taps[row : row + 1, lane] * rows[at : at + BLOCK]
    return total


def valid_rows(fill, b):
    return lax.broadcasted_iota(jnp.int32, (BLOCK, LANES), 0) < fill[b]


def forward_kernel(same, fill, units, taps, activated, slope, win, held_act, held_slope, sems):
    def stores(lane, c):
        return (
            pltpu.make_async_copy(held_act.at[:, lane], activated.at[:, lane], sems.at[0, c]),
            pltpu.make_async_copy(held_slope.at[:, lane], slope.at[:, lane], sems.at[1, c]),
        )

    def step(lane, c):
        fill_extended(win, units, same, lane)
        for b in range(win.shape[0]):
            conv = convolve(win, b, taps, lane, False)
            q = jax.nn.sigmoid(conv)
            valid = valid_rows(fill, b)
            rows = slice(b * BLOCK, (b + 1) * BLOCK)
            held_act[rows, lane] = jnp.where(valid, conv * q, 0.0).astype(BF16)
            held_slope[rows, lane] = jnp.where(valid, q + conv * q * (1.0 - q), 0.0)
        for copy in stores(lane, c):
            copy.start()

    each_lane_block(units.shape[1], step)
    for c in range(units.shape[1] // LANES):
        for copy in stores(pl.ds(c * LANES, LANES), c):
            copy.wait()


def taps_kernel(same, units, grad_conv, out, win, sums):
    def step(lane, c):
        fill_extended(win, units, same, lane)
        sums[...] = jnp.zeros_like(sums)
        for b in range(win.shape[0]):
            grad = grad_conv[b * BLOCK : (b + 1) * BLOCK, lane]
            for shift in range(8):
                steps, rows = shifted(win, b, shift)
                for k, at in steps:
                    terms = (rows[at : at + BLOCK] * grad).reshape(BLOCK // 8, 8, LANES)
                    sums[k] += jnp.sum(terms, axis=0)
        out[:, lane] = jnp.sum(sums[...], axis=1)

    each_lane_block(units.shape[1], step)


def backward_kernel(same, fill, grad_conv, inner, outer, taps, value, gate, out, win):
    def step(lane, c):
        fill_windows(win, grad_conv, inner, outer, same, lane)
        for b in range(win.shape[0]):
            grad_units = jnp.where(valid_rows(fill, b), convolve(win, b, taps, lane, True), 0.0)
            rows = slice(b * BLOCK, (b + 1) * BLOCK)
            own = slice(b * BLOCK + HALO, (b + 1) * BLOCK + HALO)
            s = gate[own, lane]
            grad_value = grad_units * s
            out[0, rows, lane] = grad_value.astype(BF16)
            out[1, rows, lane] = (grad_value * value[own, lane] * (1.0 - s)).astype(BF16)

    each_lane_block(grad_conv.shape[1], step)


def norm_kernel(place, frames, inner, outer, gain, out, out_t):
    def rows(block):
        x = block.astype(F32)
        center = x - jnp.mean(x, axis=1, keepdims=True)
        inv = lax.rsqrt(jnp.mean(center * center, axis=1, keepdims=True) + EPSILON)
        return (center * inv * gain[...]).astype(BF16)

    for first in range(0, frames.shape[0], BLOCK):
        normed = rows(frames[first : first + BLOCK, :])
        out[HALO + first : HALO + first + BLOCK, :] = normed
        out_t[:, first : first + BLOCK] = normed.T
    odd = place[2] % 2 == 1
    out[:HALO, :] = rows(jnp.where(odd, inner[...].astype(F32), outer[...].astype(F32)))
    out[out.shape[0] - HALO :, :] = rows(jnp.where(odd, outer[...].astype(F32), inner[...].astype(F32)))


def chunks_kernel(section, rows, *refs):
    outs, held, sems = refs[:4], refs[4], refs[5]
    count = held.shape[2]
    loads, stores = [], []
    for k, out in enumerate(outs):
        first = pl.multiple_of((section[0] ^ k) * count, count)
        loads.append(pltpu.make_async_copy(rows.at[:, pl.ds(first, count)], held.at[k], sems.at[0, k]))
        stores.append(pltpu.make_async_copy(held.at[k], out, sems.at[1, k]))
    for load in loads[1:] + loads[:1]:
        load.start()
    for k in (1, 2, 3, 0):
        loads[k].wait()
        stores[k].start()
    for store in stores:
        store.wait()


def gradient_kernel(section, own, first, second, third, weights, slope, arrived, out, sems):
    pieces = own, first, second, third
    rows = own.shape[0]
    copies = []
    for k, piece in enumerate(pieces):
        at = pl.multiple_of((section[0] ^ k) * rows, 64)
        copies.append(pltpu.make_async_copy(piece, arrived.at[pl.ds(at, rows), :], sems.at[k]))
    for copy in copies:
        copy.start()
    for copy in copies:
        copy.wait()
    grad = jnp.dot(weights[...], arrived[...], preferred_element_type=F32)
    out[...] = grad.T * slope[...]


def halves_kernel(core, rows, order, own, other, held, sem):
    copy = pltpu.make_async_copy(held, other, sem)
    for half, out in ((1 - core[0], held), (core[0], own)):
        for y in range(4):
            first = pl.multiple_of(y * 160 + half * 80, 16)
            second = pl.multiple_of((4 + y) * 160 + half * 80, 16)
            both = jnp.concatenate([rows[pl.ds(first, 80), :], rows[pl.ds(second, 80), :]], axis=0)
            moved = jnp.dot(order[...], both, preferred_element_type=F32)
            out[y * 160 : (y + 1) * 160, :] = moved.astype(BF16)
        if out is held:
            copy.start()
    copy.wait()


def final_kernel(sent, other, frames, arrived, gain, out):
    x = frames[...].astype(F32)
    center = x - jnp.mean(x, axis=1, keepdims=True)
    inv = lax.rsqrt(jnp.mean(center * center, axis=1, keepdims=True) + EPSILON)
    unit = center * inv
    e = (sent[...].astype(F32) + other[...].astype(F32)) * gain[...]
    back = e - jnp.mean(e, axis=1, keepdims=True) - unit * jnp.mean(e * unit, axis=1, keepdims=True)
    out[...] = (arrived[...].astype(F32).T + inv * back).astype(BF16)


def pair_kernel(first, left, left_peer, right, right_peer, *refs):
    out, held, sems = refs[-3:]
    groups, _, width = right.shape
    copies = []
    for g in range(groups):
        for at in range(0, width, 256):
            columns = slice(at, min(at + 256, width))
            total = jnp.dot(left[...], right[g, :, columns], preferred_element_type=F32)
            total = total + jnp.dot(left_peer[...], right_peer[g, :, columns], preferred_element_type=F32)
            made = pl.ds(g * width + at, columns.stop - at)
            held[:, made] = total.astype(BF16)
            there = pl.ds((first + g) * width + at, columns.stop - at)
            copies.append(pltpu.make_async_copy(held.at[:, made], out.at[:, there], sems.at[len(copies)]))
            copies[-1].start()
    for copy in copies:
        copy.wait()


def hbm():
    return pl.BlockSpec(memory_space=pltpu.HBM)


def smem():
    return pl.BlockSpec(memory_space=pltpu.SMEM)


def vmem():
    return pl.BlockSpec(memory_space=pltpu.VMEM)


def windows(count):
    return pltpu.VMEM((count // BLOCK, BLOCK + 2 * HALO, LANES), F32)


def convolved(same, fill, units, taps, count):
    width = units.shape[1]
    return pl.pallas_call(
        forward_kernel,
        in_specs=[smem(), smem(), vmem(), vmem()],
        out_specs=[hbm(), hbm()],
        out_shape=[pltpu.HBM((count, width), BF16), pltpu.HBM((count, width), F32)],
        scratch_shapes=[
            windows(count),
            pltpu.VMEM((count, width), BF16),
            pltpu.VMEM((count, width), F32),
            pltpu.SemaphoreType.DMA((2, width // LANES)),
        ],
        compiler_params=params(),
        cost_estimate=duration(5),
        name="conv_forward",
    )(same, fill, units, taps)


def tap_sums(same, units, grad_conv):
    count, width = grad_conv.shape
    return pl.pallas_call(
        taps_kernel,
        in_specs=[smem(), vmem(), vmem()],
        out_specs=vmem(),
        out_shape=jax.ShapeDtypeStruct((32, width), F32),
        scratch_shapes=[windows(count), pltpu.VMEM((32, 8, LANES), F32)],
        compiler_params=params(),
        cost_estimate=duration(4),
        name="tap_gradients",
    )(same, units, grad_conv)


def projected_back(same, fill, grad_conv, inner, outer, taps, value, gate):
    count, width = grad_conv.shape
    return pl.pallas_call(
        backward_kernel,
        in_specs=[smem(), smem()] + [vmem()] * 6,
        out_specs=vmem(),
        out_shape=jax.ShapeDtypeStruct((2, count, width), BF16),
        scratch_shapes=[windows(count)],
        compiler_params=params(),
        cost_estimate=duration(5.6),
        name="conv_backward",
    )(same, fill, grad_conv, inner, outer, taps, value, gate)


def normalised(place, frames, inner, outer, gain):
    count, features = frames.shape
    return pl.pallas_call(
        norm_kernel,
        in_specs=[smem()] + [vmem()] * 4,
        out_specs=[vmem(), vmem()],
        out_shape=[
            jax.ShapeDtypeStruct((count + 2 * HALO, features), BF16),
            jax.ShapeDtypeStruct((features, count), BF16),
        ],
        compiler_params=params(),
        cost_estimate=duration(3.5),
        name="layer_norm",
    )(place, frames, inner, outer, gain.reshape(1, features))


def frame_chunks(section, rows):
    features, total = rows.shape
    count = total // 4
    return pl.pallas_call(
        chunks_kernel,
        in_specs=[smem(), hbm()],
        out_specs=[hbm()] * 4,
        out_shape=[pltpu.HBM((features, count), rows.dtype)] * 4,
        scratch_shapes=[pltpu.VMEM((4, features, count), rows.dtype), pltpu.SemaphoreType.DMA((2, 4))],
        compiler_params=params(),
        cost_estimate=duration(2),
        name="frame_chunks",
    )(section, in_hbm(rows))


def conv_gradient(section, pieces, weights, slope):
    features, count = 4 * pieces[0].shape[0], pieces[0].shape[1]
    return pl.pallas_call(
        gradient_kernel,
        in_specs=[smem()] + [hbm()] * 4 + [vmem()] * 2,
        out_specs=[vmem()] * 2,
        out_shape=[
            jax.ShapeDtypeStruct((features, count), BF16),
            jax.ShapeDtypeStruct((count, weights.shape[0]), F32),
        ],
        scratch_shapes=[pltpu.SemaphoreType.DMA((4,))],
        compiler_params=params(),
        cost_estimate=duration(3),
        name="conv_gradient",
    )(section, *[in_hbm(piece) for piece in pieces], weights, slope)


def halves(core, rows, keep=False):
    features, count = rows.shape
    order = np.zeros((160, 160), np.float32)
    for z in range(4):
        for x in range(2):
            for r in range(20):
                order[(z * 2 + x) * 20 + r, x * 80 + z * 20 + r] = 1.0
    half = jax.ShapeDtypeStruct((features // 2, count), BF16)
    return pl.pallas_call(
        halves_kernel,
        in_specs=[smem(), vmem(), vmem()],
        out_specs=[vmem(), hbm()],
        out_shape=[half if keep else pltpu.HBM(half.shape, BF16), pltpu.HBM(half.shape, BF16)],
        scratch_shapes=[pltpu.VMEM(half.shape, BF16), pltpu.SemaphoreType.DMA],
        compiler_params=params(),
        cost_estimate=duration(1.2),
        name="core_halves",
    )(core.reshape(1), rows, jnp.asarray(order, BF16))


def norm_back(sent, other, frames, arrived, gain):
    count, features = frames.shape
    block = pl.BlockSpec((BLOCK, features), lambda i: (i, 0))
    return pl.pallas_call(
        final_kernel,
        grid=(count // BLOCK,),
        in_specs=[
            block,
            block,
            block,
            pl.BlockSpec((features, BLOCK), lambda i: (0, i)),
            pl.BlockSpec((1, features), lambda i: (0, 0)),
        ],
        out_specs=block,
        out_shape=jax.ShapeDtypeStruct((count, features), BF16),
        compiler_params=params(),
        cost_estimate=duration(10.4),
        name="norm_backward",
    )(in_hbm(sent), in_hbm(other), in_hbm(frames), in_hbm(arrived), gain)


def pair_product(left, left_peer, right, right_peer, groups, first, buffer=None):
    rows = left.shape[0]
    made, _, width = right.shape
    return pl.pallas_call(
        functools.partial(pair_kernel, first),
        in_specs=[vmem()] * 4 + ([] if buffer is None else [hbm()]),
        out_specs=hbm(),
        out_shape=pltpu.HBM((rows, groups * width), BF16),
        scratch_shapes=[pltpu.VMEM((rows, made * width), BF16), pltpu.SemaphoreType.DMA((3 * made,))],
        input_output_aliases={} if buffer is None else {4: 0},
        compiler_params=params(),
        cost_estimate=duration(3.4),
        name="weight_gradient",
    )(left, left_peer, right, right_peer, *([] if buffer is None else [in_hbm(buffer)]))


def shares_of(value, axis):
    return [value] + [lax.ppermute(value, axis, [(i, i ^ k) for i in range(4)]) for k in (1, 2, 3)]


def sum_of(shares):
    own, first, second, third = [share.astype(F32) for share in shares]
    return (own + first) + (second + third)


def finish_rows(summed, xl):
    own = lax.dynamic_index_in_dim(summed, xl, 0, keepdims=False)
    other = lax.dynamic_index_in_dim(summed, 1 - xl, 0, keepdims=False)
    return own + swap(other.astype(BF16), "xl").astype(F32)


def body(frames, returned, norm_gain, weight_in, kernel, weight_out, block_utt, block_fill):
    count = frames.shape[0]
    width = weight_in.shape[2]
    features = frames.shape[1]
    blocks = count // BLOCK
    core, xl = lax.axis_index("core"), lax.axis_index("xl")
    first_block = lax.axis_index(FRAMES) * blocks
    place = jnp.stack([core, lax.axis_index("y"), lax.axis_index("section")]).astype(jnp.int32)
    section = lax.axis_index("section").reshape(1)
    *chunks, frames = lax.optimization_barrier((*frame_chunks(section, returned.T), frames))
    for k in (1, 3, 2):
        chunks[k] = lax.ppermute(chunks[k], "section", [(i, i ^ k) for i in range(4)])

    edge = jnp.full((1,), -1, jnp.int32)
    near_utt = lax.dynamic_slice(jnp.concatenate([edge, block_utt, edge]), (first_block,), (blocks + 2,))
    near_fill = lax.dynamic_slice(jnp.concatenate([edge, block_fill, edge]), (first_block,), (blocks + 2,))
    same = (near_utt[1:] == near_utt[:-1]).astype(jnp.int32)
    same = jnp.concatenate([same, lax.axis_index(FRAMES)[None].astype(jnp.int32) % 2])
    fill = near_fill[1:-1]
    valid = (jnp.arange(BLOCK, dtype=jnp.int32)[None, :] < near_fill[:, None]).reshape(-1)
    valid = valid[BLOCK - HALO : BLOCK + count + HALO]

    normed_ext, normed_t = normalised(place, frames, *halos(frames), norm_gain)
    value_proj = jnp.dot(normed_ext, weight_in[0], preferred_element_type=F32)
    gate_proj = jnp.dot(normed_ext, weight_in[1], preferred_element_type=F32)
    gate_sigmoid = jax.nn.sigmoid(gate_proj)
    units = jnp.where(valid[:, None], value_proj * gate_sigmoid, 0.0).astype(BF16)
    activated, slope = convolved(same, fill, units, kernel, count)
    activated_peer = swap(activated, "core")

    normed_own, normed_other = halves(core, normed_t)
    normed_peer = swap(normed_other, "core")

    arrived, grad_conv = conv_gradient(section, chunks, weight_out, slope)
    normed_own, normed_other, grad_conv = lax.optimization_barrier((normed_own, normed_other, grad_conv))
    conv_inner, conv_outer = halos(grad_conv)
    arrived_rows, grad_conv = lax.optimization_barrier((arrived, grad_conv))
    rows_own, rows_other = halves(core, arrived_rows, keep=True)
    rows_peer = swap(rows_other, "core")
    parts = pair_product(rows_own, rows_peer, activated[None], activated_peer[None], 3, 0)

    ready, parts = lax.optimization_barrier((grad_conv, parts))
    late = projected_back(
        same, fill, ready, conv_inner, conv_outer, kernel, value_proj, gate_sigmoid
    )
    late_peer = swap(late, "core")
    contract = (((0, 2), (0, 2)), ((), ()))
    sent = lax.dot_general(late, weight_in, contract, preferred_element_type=F32).astype(BF16)
    other = swap(sent, "tensor")
    late, sent = lax.optimization_barrier((late, sent))
    parts = pair_product(normed_own, normed_peer, late, late_peer, 3, 1, parts)
    got = lax.all_to_all(parts.reshape(16, 40, 3 * width), PLANE, 0, 0)

    ready, sent_again, _ = lax.optimization_barrier((grad_conv, sent, parts))
    taps_part = tap_sums(same, units, ready)
    gain_part = sent_again.astype(F32) * normed_ext[HALO : HALO + count].astype(F32)
    gain_part = jnp.sum(gain_part, axis=0) / norm_gain
    small = jnp.concatenate([taps_part, gain_part.reshape(2, width)], axis=0)
    small = small + swap(small, "core")
    gain = small[32:]
    corner = lax.ppermute(gain, ("xl", "tensor"), [(0, 3), (1, 2), (2, 1), (3, 0)])
    across = swap(small, "xl"), swap(gain, "tensor"), corner
    grad_frames = norm_back(sent, other, frames, arrived, norm_gain.reshape(1, features))
    small, across, grad_frames = lax.optimization_barrier((small, across, grad_frames))
    gain = (small[32:] + across[1]) + (across[0][32:] + across[2])
    small = jnp.concatenate([small[:32] + across[0][:32], gain], axis=0)
    shares = shares_of(small.astype(BF16), "y")
    got, grad_frames = lax.optimization_barrier((got, grad_frames))
    total = jnp.sum(got.astype(F32), axis=0)
    total, shares = lax.optimization_barrier((total, shares))
    summed = finish_rows(total.reshape(2, 20, 3 * width), xl)
    grad_out = summed[:, :width].T
    grad_in = summed[:, width:].reshape(20, 2, width).transpose(1, 0, 2)
    shares = shares_of(sum_of(shares).astype(BF16), "section")
    grad_in, grad_out, shares = lax.optimization_barrier((grad_in, grad_out, shares))
    small = sum_of(shares)
    grad_kernel = small[:TAPS]
    grad_gain = small[32:].reshape(features)
    return (grad_frames, grad_in, grad_out, grad_kernel, grad_gain)


def solution(mesh):
    split = Mesh(
        np.asarray(mesh.devices).reshape(2, 4, 2, 2, 4), ("xl", "y", "core", "tensor", "section")
    )
    outer = ("xl", "y", "core")
    in_specs = (
        P(FRAMES, None),
        P(outer, "section"),
        P(),
        P(None, None, "tensor"),
        P(None, "tensor"),
        P("tensor", None),
        P(),
        P(),
    )
    out_specs = (
        P(FRAMES, None),
        P(None, FRAMES, "tensor"),
        P("tensor", FRAMES),
        P(None, "tensor"),
        P(),
    )
    return jax.shard_map(body, mesh=split, in_specs=in_specs, out_specs=out_specs, check_vma=False)
```

```python
import functools

import jax
import jax.numpy as jnp
import numpy as np
from jax import lax
from jax.experimental import pallas as pl
from jax.experimental.pallas import tpu as pltpu
from jax.sharding import Mesh
from jax.sharding import PartitionSpec as P

BLOCK = 128
HALO = 16
TAPS = 31
LANES = 128
EPSILON = 1e-05
BF16 = jnp.bfloat16
F32 = jnp.float32

FRAMES = ("xl", "y", "core", "section")
PLANE = ("y", "section")
MIB = 1024 * 1024


def params(mib=16):
    return pltpu.CompilerParams(vmem_limit_bytes=mib * MIB)


def duration(us):
    return pl.CostEstimate(flops=round(us * 1.15e9), bytes_accessed=0, transcendentals=0)


def in_hbm(array):
    return pltpu.with_memory_space_constraint(array, pltpu.HBM)


def swap(value, axis):
    return lax.ppermute(value, axis, [(0, 1), (1, 0)])


def halos(shard):
    peers = lax.axis_size(FRAMES)
    odd = lax.axis_index(FRAMES) % 2 == 1
    first, last = shard[:HALO], shard[shard.shape[0] - HALO :]
    pairs = [(i, i ^ 1) for i in range(peers)]
    across = [(i, i + 1) for i in range(1, peers - 1, 2)]
    across = across + [(j, i) for i, j in across]
    inner = lax.ppermute(jnp.where(odd, first, last), FRAMES, pairs)
    outer = lax.ppermute(jnp.where(odd, last, first), FRAMES, across)
    return inner, outer


def each_lane_block(width, step):
    def block(c, carry):
        step(pl.ds(pl.multiple_of(c * LANES, LANES), LANES), c)
        return carry

    lax.fori_loop(0, width // LANES, block, 0)


def fill_windows(win, main, inner, outer, same, lane):
    odd = same[win.shape[0] + 1] == 1
    before = jnp.where(odd, inner[:, lane], outer[:, lane])
    after = jnp.where(odd, outer[:, lane], inner[:, lane])
    blocks = win.shape[0]
    for b in range(blocks):
        lo, hi = b * BLOCK, (b + 1) * BLOCK
        prior = before if b == 0 else main[lo - HALO : lo, lane]
        later = after if b == blocks - 1 else main[hi : hi + HALO, lane]
        win[b, HALO : HALO + BLOCK, :] = main[lo:hi, lane].astype(F32)
        win[b, :HALO, :] = jnp.where(same[b] == 1, prior.astype(F32), 0.0)
        win[b, HALO + BLOCK :, :] = jnp.where(same[b + 1] == 1, later.astype(F32), 0.0)


def fill_extended(win, rows, same, lane):
    for b in range(win.shape[0]):
        lo = b * BLOCK
        hi = lo + HALO + BLOCK
        win[b, HALO : HALO + BLOCK, :] = rows[lo + HALO : hi, lane].astype(F32)
        win[b, :HALO, :] = jnp.where(same[b] == 1, rows[lo : lo + HALO, lane].astype(F32), 0.0)
        win[b, HALO + BLOCK :, :] = jnp.where(same[b + 1] == 1, rows[hi : hi + HALO, lane].astype(F32), 0.0)


def shifted(win, b, shift):
    first = 1 if shift == 0 else 0
    return [(8 * a + shift - 1, 8 * a) for a in range(first, 4)], win[b, pl.ds(shift, BLOCK + 24), :]


def convolve(win, b, taps, lane, flip):
    total = jnp.zeros((BLOCK, LANES), F32)
    for shift in range(8):
        steps, rows = shifted(win, b, shift)
        for k, at in steps:
            row = TAPS - 1 - k if flip else k
            total = total + taps[row : row + 1, lane] * rows[at : at + BLOCK]
    return total


def valid_rows(fill, b):
    return lax.broadcasted_iota(jnp.int32, (BLOCK, LANES), 0) < fill[b]


def forward_kernel(same, fill, units, taps, activated, slope, win, held_act, held_slope, sems):
    def stores(lane, c):
        return (
            pltpu.make_async_copy(held_act.at[:, lane], activated.at[:, lane], sems.at[0, c]),
            pltpu.make_async_copy(held_slope.at[:, lane], slope.at[:, lane], sems.at[1, c]),
        )

    def step(lane, c):
        fill_extended(win, units, same, lane)
        for b in range(win.shape[0]):
            conv = convolve(win, b, taps, lane, False)
            q = jax.nn.sigmoid(conv)
            valid = valid_rows(fill, b)
            rows = slice(b * BLOCK, (b + 1) * BLOCK)
            held_act[rows, lane] = jnp.where(valid, conv * q, 0.0).astype(BF16)
            held_slope[rows, lane] = jnp.where(valid, q + conv * q * (1.0 - q), 0.0)
        for copy in stores(lane, c):
            copy.start()

    each_lane_block(units.shape[1], step)
    for c in range(units.shape[1] // LANES):
        for copy in stores(pl.ds(c * LANES, LANES), c):
            copy.wait()


def taps_kernel(same, units, grad_conv, out, win, sums):
    def step(lane, c):
        fill_extended(win, units, same, lane)
        sums[...] = jnp.zeros_like(sums)
        for b in range(win.shape[0]):
            grad = grad_conv[b * BLOCK : (b + 1) * BLOCK, lane]
            for shift in range(8):
                steps, rows = shifted(win, b, shift)
                for k, at in steps:
                    terms = (rows[at : at + BLOCK] * grad).reshape(BLOCK // 8, 8, LANES)
                    sums[k] += jnp.sum(terms, axis=0)
        out[:, lane] = jnp.sum(sums[...], axis=1)

    each_lane_block(units.shape[1], step)


def backward_kernel(same, fill, grad_conv, inner, outer, taps, value, gate, out, win):
    def step(lane, c):
        fill_windows(win, grad_conv, inner, outer, same, lane)
        for b in range(win.shape[0]):
            grad_units = jnp.where(valid_rows(fill, b), convolve(win, b, taps, lane, True), 0.0)
            rows = slice(b * BLOCK, (b + 1) * BLOCK)
            own = slice(b * BLOCK + HALO, (b + 1) * BLOCK + HALO)
            s = gate[own, lane]
            grad_value = grad_units * s
            out[0, rows, lane] = grad_value.astype(BF16)
            out[1, rows, lane] = (grad_value * value[own, lane] * (1.0 - s)).astype(BF16)

    each_lane_block(grad_conv.shape[1], step)


def norm_kernel(place, frames, inner, outer, gain, out, out_t):
    def rows(block):
        x = block.astype(F32)
        center = x - jnp.mean(x, axis=1, keepdims=True)
        inv = lax.rsqrt(jnp.mean(center * center, axis=1, keepdims=True) + EPSILON)
        return (center * inv * gain[...]).astype(BF16)

    for first in range(0, frames.shape[0], BLOCK):
        normed = rows(frames[first : first + BLOCK, :])
        out[HALO + first : HALO + first + BLOCK, :] = normed
        out_t[:, first : first + BLOCK] = normed.T
    odd = place[2] % 2 == 1
    out[:HALO, :] = rows(jnp.where(odd, inner[...].astype(F32), outer[...].astype(F32)))
    out[out.shape[0] - HALO :, :] = rows(jnp.where(odd, outer[...].astype(F32), inner[...].astype(F32)))


def chunks_kernel(section, rows, *refs):
    outs, held, sems = refs[:3], refs[3], refs[4]
    count = held.shape[2]
    loads, stores = [], []
    for i, out in enumerate(outs):
        first = pl.multiple_of((section[0] ^ (i + 1)) * count, count)
        loads.append(pltpu.make_async_copy(rows.at[:, pl.ds(first, count)], held.at[i], sems.at[0, i]))
        stores.append(pltpu.make_async_copy(held.at[i], out, sems.at[1, i]))
    for load in loads:
        load.start()
    for load, store in zip(loads, stores):
        load.wait()
        store.start()
    for store in stores:
        store.wait()


def gradient_kernel(section, own, first, second, third, weights, slope, arrived, out, sems):
    rows, count = first.shape
    here = pl.multiple_of(section[0] * count, count)
    pieces = own.at[:, pl.ds(here, count)], first, second, third
    copies = []
    for k, piece in enumerate(pieces):
        at = pl.multiple_of((section[0] ^ k) * rows, 64)
        copies.append(pltpu.make_async_copy(piece, arrived.at[pl.ds(at, rows), :], sems.at[k]))
    for copy in copies:
        copy.start()
    for copy in copies:
        copy.wait()
    grad = jnp.dot(weights[...], arrived[...], preferred_element_type=F32)
    out[...] = grad.T * slope[...]


def halves_kernel(core, rows, order, own, other, held, sem):
    copy = pltpu.make_async_copy(held, other, sem)
    for half, out in ((1 - core[0], held), (core[0], own)):
        for y in range(4):
            first = pl.multiple_of(y * 160 + half * 80, 16)
            second = pl.multiple_of((4 + y) * 160 + half * 80, 16)
            both = jnp.concatenate([rows[pl.ds(first, 80), :], rows[pl.ds(second, 80), :]], axis=0)
            moved = jnp.dot(order[...], both, preferred_element_type=F32)
            out[y * 160 : (y + 1) * 160, :] = moved.astype(BF16)
        if out is held:
            copy.start()
    copy.wait()


def final_kernel(sent, other, frames, arrived, gain, out):
    x = frames[...].astype(F32)
    center = x - jnp.mean(x, axis=1, keepdims=True)
    inv = lax.rsqrt(jnp.mean(center * center, axis=1, keepdims=True) + EPSILON)
    unit = center * inv
    e = (sent[...].astype(F32) + other[...].astype(F32)) * gain[...]
    back = e - jnp.mean(e, axis=1, keepdims=True) - unit * jnp.mean(e * unit, axis=1, keepdims=True)
    out[...] = (arrived[...].astype(F32).T + inv * back).astype(BF16)


def pair_kernel(first, left, left_peer, right, right_peer, *refs):
    out, held, sems = refs[-3:]
    groups, _, width = right.shape
    copies = []
    for g in range(groups):
        for at in range(0, width, 256):
            columns = slice(at, min(at + 256, width))
            total = jnp.dot(left[...], right[g, :, columns], preferred_element_type=F32)
            total = total + jnp.dot(left_peer[...], right_peer[g, :, columns], preferred_element_type=F32)
            made = pl.ds(g * width + at, columns.stop - at)
            held[:, made] = total.astype(BF16)
            there = pl.ds((first + g) * width + at, columns.stop - at)
            copies.append(pltpu.make_async_copy(held.at[:, made], out.at[:, there], sems.at[len(copies)]))
            copies[-1].start()
    for copy in copies:
        copy.wait()


def hbm():
    return pl.BlockSpec(memory_space=pltpu.HBM)


def smem():
    return pl.BlockSpec(memory_space=pltpu.SMEM)


def vmem():
    return pl.BlockSpec(memory_space=pltpu.VMEM)


def windows(count):
    return pltpu.VMEM((count // BLOCK, BLOCK + 2 * HALO, LANES), F32)


def convolved(same, fill, units, taps, count):
    width = units.shape[1]
    return pl.pallas_call(
        forward_kernel,
        in_specs=[smem(), smem(), vmem(), vmem()],
        out_specs=[hbm(), hbm()],
        out_shape=[pltpu.HBM((count, width), BF16), pltpu.HBM((count, width), F32)],
        scratch_shapes=[
            windows(count),
            pltpu.VMEM((count, width), BF16),
            pltpu.VMEM((count, width), F32),
            pltpu.SemaphoreType.DMA((2, width // LANES)),
        ],
        compiler_params=params(),
        cost_estimate=duration(5),
        name="conv_forward",
    )(same, fill, units, taps)


def tap_sums(same, units, grad_conv):
    count, width = grad_conv.shape
    return pl.pallas_call(
        taps_kernel,
        in_specs=[smem(), vmem(), vmem()],
        out_specs=vmem(),
        out_shape=jax.ShapeDtypeStruct((32, width), F32),
        scratch_shapes=[windows(count), pltpu.VMEM((32, 8, LANES), F32)],
        compiler_params=params(),
        cost_estimate=duration(4),
        name="tap_gradients",
    )(same, units, grad_conv)


def projected_back(same, fill, grad_conv, inner, outer, taps, value, gate):
    count, width = grad_conv.shape
    return pl.pallas_call(
        backward_kernel,
        in_specs=[smem(), smem()] + [vmem()] * 6,
        out_specs=vmem(),
        out_shape=jax.ShapeDtypeStruct((2, count, width), BF16),
        scratch_shapes=[windows(count)],
        compiler_params=params(),
        cost_estimate=duration(5.6),
        name="conv_backward",
    )(same, fill, grad_conv, inner, outer, taps, value, gate)


def normalised(place, frames, inner, outer, gain):
    count, features = frames.shape
    return pl.pallas_call(
        norm_kernel,
        in_specs=[smem()] + [vmem()] * 4,
        out_specs=[vmem(), vmem()],
        out_shape=[
            jax.ShapeDtypeStruct((count + 2 * HALO, features), BF16),
            jax.ShapeDtypeStruct((features, count), BF16),
        ],
        compiler_params=params(),
        cost_estimate=duration(3.5),
        name="layer_norm",
    )(place, frames, inner, outer, gain.reshape(1, features))


def frame_chunks(section, rows):
    features, total = rows.shape
    count = total // 4
    return pl.pallas_call(
        chunks_kernel,
        in_specs=[smem(), hbm()],
        out_specs=[hbm()] * 3,
        out_shape=[pltpu.HBM((features, count), rows.dtype)] * 3,
        scratch_shapes=[pltpu.VMEM((3, features, count), rows.dtype), pltpu.SemaphoreType.DMA((2, 3))],
        compiler_params=params(),
        cost_estimate=duration(2),
        name="frame_chunks",
    )(section, in_hbm(rows))


def conv_gradient(section, pieces, weights, slope):
    features, count = 4 * pieces[1].shape[0], pieces[1].shape[1]
    return pl.pallas_call(
        gradient_kernel,
        in_specs=[smem()] + [hbm()] * 4 + [vmem()] * 2,
        out_specs=[vmem()] * 2,
        out_shape=[
            jax.ShapeDtypeStruct((features, count), BF16),
            jax.ShapeDtypeStruct((count, weights.shape[0]), F32),
        ],
        scratch_shapes=[pltpu.SemaphoreType.DMA((4,))],
        compiler_params=params(),
        cost_estimate=duration(3),
        name="conv_gradient",
    )(section, *[in_hbm(piece) for piece in pieces], weights, slope)


def halves(core, rows, keep=False):
    features, count = rows.shape
    order = np.zeros((160, 160), np.float32)
    for z in range(4):
        for x in range(2):
            for r in range(20):
                order[(z * 2 + x) * 20 + r, x * 80 + z * 20 + r] = 1.0
    half = jax.ShapeDtypeStruct((features // 2, count), BF16)
    return pl.pallas_call(
        halves_kernel,
        in_specs=[smem(), vmem(), vmem()],
        out_specs=[vmem(), hbm()],
        out_shape=[half if keep else pltpu.HBM(half.shape, BF16), pltpu.HBM(half.shape, BF16)],
        scratch_shapes=[pltpu.VMEM(half.shape, BF16), pltpu.SemaphoreType.DMA],
        compiler_params=params(),
        cost_estimate=duration(1.2),
        name="core_halves",
    )(core.reshape(1), rows, jnp.asarray(order, BF16))


def norm_back(sent, other, frames, arrived, gain):
    count, features = frames.shape
    block = pl.BlockSpec((BLOCK, features), lambda i: (i, 0))
    return pl.pallas_call(
        final_kernel,
        grid=(count // BLOCK,),
        in_specs=[
            block,
            block,
            block,
            pl.BlockSpec((features, BLOCK), lambda i: (0, i)),
            pl.BlockSpec((1, features), lambda i: (0, 0)),
        ],
        out_specs=block,
        out_shape=jax.ShapeDtypeStruct((count, features), BF16),
        compiler_params=params(),
        cost_estimate=duration(10.4),
        name="norm_backward",
    )(in_hbm(sent), in_hbm(other), in_hbm(frames), in_hbm(arrived), gain)


def pair_product(left, left_peer, right, right_peer, groups, first, buffer=None):
    rows = left.shape[0]
    made, _, width = right.shape
    return pl.pallas_call(
        functools.partial(pair_kernel, first),
        in_specs=[vmem()] * 4 + ([] if buffer is None else [hbm()]),
        out_specs=hbm(),
        out_shape=pltpu.HBM((rows, groups * width), BF16),
        scratch_shapes=[pltpu.VMEM((rows, made * width), BF16), pltpu.SemaphoreType.DMA((3 * made,))],
        input_output_aliases={} if buffer is None else {4: 0},
        compiler_params=params(),
        cost_estimate=duration(3.4),
        name="weight_gradient",
    )(left, left_peer, right, right_peer, *([] if buffer is None else [in_hbm(buffer)]))


def shares_of(value, axis):
    return [value] + [lax.ppermute(value, axis, [(i, i ^ k) for i in range(4)]) for k in (1, 2, 3)]


def sum_of(shares):
    own, first, second, third = [share.astype(F32) for share in shares]
    return (own + first) + (second + third)


def finish_rows(summed, xl):
    own = lax.dynamic_index_in_dim(summed, xl, 0, keepdims=False)
    other = lax.dynamic_index_in_dim(summed, 1 - xl, 0, keepdims=False)
    return own + swap(other.astype(BF16), "xl").astype(F32)


def body(frames, returned, norm_gain, weight_in, kernel, weight_out, block_utt, block_fill):
    count = frames.shape[0]
    width = weight_in.shape[2]
    features = frames.shape[1]
    blocks = count // BLOCK
    core, xl = lax.axis_index("core"), lax.axis_index("xl")
    first_block = lax.axis_index(FRAMES) * blocks
    place = jnp.stack([core, lax.axis_index("y"), lax.axis_index("section")]).astype(jnp.int32)
    section = lax.axis_index("section").reshape(1)
    *chunks, frames = lax.optimization_barrier((*frame_chunks(section, returned.T), frames))
    pieces = [returned.T]
    for k, chunk in enumerate(chunks, 1):
        pieces.append(lax.ppermute(chunk, "section", [(i, i ^ k) for i in range(4)]))

    edge = jnp.full((1,), -1, jnp.int32)
    near_utt = lax.dynamic_slice(jnp.concatenate([edge, block_utt, edge]), (first_block,), (blocks + 2,))
    near_fill = lax.dynamic_slice(jnp.concatenate([edge, block_fill, edge]), (first_block,), (blocks + 2,))
    same = (near_utt[1:] == near_utt[:-1]).astype(jnp.int32)
    same = jnp.concatenate([same, lax.axis_index(FRAMES)[None].astype(jnp.int32) % 2])
    fill = near_fill[1:-1]
    valid = (jnp.arange(BLOCK, dtype=jnp.int32)[None, :] < near_fill[:, None]).reshape(-1)
    valid = valid[BLOCK - HALO : BLOCK + count + HALO]

    normed_ext, normed_t = normalised(place, frames, *halos(frames), norm_gain)
    value_proj = jnp.dot(normed_ext, weight_in[0], preferred_element_type=F32)
    gate_proj = jnp.dot(normed_ext, weight_in[1], preferred_element_type=F32)
    gate_sigmoid = jax.nn.sigmoid(gate_proj)
    units = jnp.where(valid[:, None], value_proj * gate_sigmoid, 0.0).astype(BF16)
    activated, slope = convolved(same, fill, units, kernel, count)
    activated_peer = swap(activated, "core")

    normed_own, normed_other = halves(core, normed_t)
    normed_peer = swap(normed_other, "core")

    arrived, grad_conv = conv_gradient(section, pieces, weight_out, slope)
    normed_own, normed_other, grad_conv = lax.optimization_barrier((normed_own, normed_other, grad_conv))
    conv_inner, conv_outer = halos(grad_conv)
    arrived_rows, grad_conv = lax.optimization_barrier((arrived, grad_conv))
    rows_own, rows_other = halves(core, arrived_rows, keep=True)
    rows_peer = swap(rows_other, "core")
    parts = pair_product(rows_own, rows_peer, activated[None], activated_peer[None], 3, 0)

    ready, parts = lax.optimization_barrier((grad_conv, parts))
    late = projected_back(
        same, fill, ready, conv_inner, conv_outer, kernel, value_proj, gate_sigmoid
    )
    late_peer = swap(late, "core")
    contract = (((0, 2), (0, 2)), ((), ()))
    sent = lax.dot_general(late, weight_in, contract, preferred_element_type=F32).astype(BF16)
    other = swap(sent, "tensor")
    late, sent = lax.optimization_barrier((late, sent))
    parts = pair_product(normed_own, normed_peer, late, late_peer, 3, 1, parts)
    got = lax.all_to_all(parts.reshape(16, 40, 3 * width), PLANE, 0, 0)

    ready, sent_again, _ = lax.optimization_barrier((grad_conv, sent, parts))
    taps_part = tap_sums(same, units, ready)
    gain_part = sent_again.astype(F32) * normed_ext[HALO : HALO + count].astype(F32)
    gain_part = jnp.sum(gain_part, axis=0) / norm_gain
    small = jnp.concatenate([taps_part, gain_part.reshape(2, width)], axis=0)
    small = small + swap(small, "core")
    gain = small[32:]
    corner = lax.ppermute(gain, ("xl", "tensor"), [(0, 3), (1, 2), (2, 1), (3, 0)])
    across = swap(small, "xl"), swap(gain, "tensor"), corner
    grad_frames = norm_back(sent, other, frames, arrived, norm_gain.reshape(1, features))
    small, across, grad_frames = lax.optimization_barrier((small, across, grad_frames))
    gain = (small[32:] + across[1]) + (across[0][32:] + across[2])
    small = jnp.concatenate([small[:32] + across[0][:32], gain], axis=0)
    shares = shares_of(small.astype(BF16), "y")
    got, grad_frames = lax.optimization_barrier((got, grad_frames))
    total = jnp.sum(got.astype(F32), axis=0)
    total, shares = lax.optimization_barrier((total, shares))
    summed = finish_rows(total.reshape(2, 20, 3 * width), xl)
    grad_out = summed[:, :width].T
    grad_in = summed[:, width:].reshape(20, 2, width).transpose(1, 0, 2)
    shares = shares_of(sum_of(shares).astype(BF16), "section")
    grad_in, grad_out, shares = lax.optimization_barrier((grad_in, grad_out, shares))
    small = sum_of(shares)
    grad_kernel = small[:TAPS]
    grad_gain = small[32:].reshape(features)
    return (grad_frames, grad_in, grad_out, grad_kernel, grad_gain)


def solution(mesh):
    split = Mesh(
        np.asarray(mesh.devices).reshape(2, 4, 2, 2, 4), ("xl", "y", "core", "tensor", "section")
    )
    outer = ("xl", "y", "core")
    in_specs = (
        P(FRAMES, None),
        P(outer, "section"),
        P(),
        P(None, None, "tensor"),
        P(None, "tensor"),
        P("tensor", None),
        P(),
        P(),
    )
    out_specs = (
        P(FRAMES, None),
        P(None, FRAMES, "tensor"),
        P("tensor", FRAMES),
        P(None, "tensor"),
        P(),
    )
    return jax.shard_map(body, mesh=split, in_specs=in_specs, out_specs=out_specs, check_vma=False)
```

```python
import functools

import jax
import jax.numpy as jnp
import numpy as np
from jax import lax
from jax.experimental import pallas as pl
from jax.experimental.pallas import tpu as pltpu
from jax.sharding import Mesh
from jax.sharding import PartitionSpec as P

BLOCK = 128
HALO = 16
TAPS = 31
LANES = 128
EPSILON = 1e-05
BF16 = jnp.bfloat16
F32 = jnp.float32

FRAMES = ("xl", "y", "core", "section")
PLANE = ("y", "section")
MIB = 1024 * 1024


def params(mib=16):
    return pltpu.CompilerParams(vmem_limit_bytes=mib * MIB)


def duration(us):
    return pl.CostEstimate(flops=round(us * 1.15e9), bytes_accessed=0, transcendentals=0)


def in_hbm(array):
    return pltpu.with_memory_space_constraint(array, pltpu.HBM)


def swap(value, axis):
    return lax.ppermute(value, axis, [(0, 1), (1, 0)])


def halos(shard):
    peers = lax.axis_size(FRAMES)
    odd = lax.axis_index(FRAMES) % 2 == 1
    first, last = shard[:HALO], shard[shard.shape[0] - HALO :]
    pairs = [(i, i ^ 1) for i in range(peers)]
    across = [(i, i + 1) for i in range(1, peers - 1, 2)]
    across = across + [(j, i) for i, j in across]
    inner = lax.ppermute(jnp.where(odd, first, last), FRAMES, pairs)
    outer = lax.ppermute(jnp.where(odd, last, first), FRAMES, across)
    return inner, outer


def each_lane_block(width, step):
    def block(c, carry):
        step(pl.ds(pl.multiple_of(c * LANES, LANES), LANES), c)
        return carry

    lax.fori_loop(0, width // LANES, block, 0)


def fill_windows(win, main, inner, outer, same, lane):
    odd = same[win.shape[0] + 1] == 1
    before = jnp.where(odd, inner[:, lane], outer[:, lane])
    after = jnp.where(odd, outer[:, lane], inner[:, lane])
    blocks = win.shape[0]
    for b in range(blocks):
        lo, hi = b * BLOCK, (b + 1) * BLOCK
        prior = before if b == 0 else main[lo - HALO : lo, lane]
        later = after if b == blocks - 1 else main[hi : hi + HALO, lane]
        win[b, HALO : HALO + BLOCK, :] = main[lo:hi, lane].astype(F32)
        win[b, :HALO, :] = jnp.where(same[b] == 1, prior.astype(F32), 0.0)
        win[b, HALO + BLOCK :, :] = jnp.where(same[b + 1] == 1, later.astype(F32), 0.0)


def fill_extended(win, rows, same, lane):
    for b in range(win.shape[0]):
        lo = b * BLOCK
        hi = lo + HALO + BLOCK
        win[b, HALO : HALO + BLOCK, :] = rows[lo + HALO : hi, lane].astype(F32)
        win[b, :HALO, :] = jnp.where(same[b] == 1, rows[lo : lo + HALO, lane].astype(F32), 0.0)
        win[b, HALO + BLOCK :, :] = jnp.where(same[b + 1] == 1, rows[hi : hi + HALO, lane].astype(F32), 0.0)


def shifted(win, b, shift):
    first = 1 if shift == 0 else 0
    return [(8 * a + shift - 1, 8 * a) for a in range(first, 4)], win[b, pl.ds(shift, BLOCK + 24), :]


def convolve(win, b, taps, lane, flip):
    total = jnp.zeros((BLOCK, LANES), F32)
    for shift in range(8):
        steps, rows = shifted(win, b, shift)
        for k, at in steps:
            row = TAPS - 1 - k if flip else k
            total = total + taps[row : row + 1, lane] * rows[at : at + BLOCK]
    return total


def valid_rows(fill, b):
    return lax.broadcasted_iota(jnp.int32, (BLOCK, LANES), 0) < fill[b]


def forward_kernel(same, fill, units, taps, activated, slope, win, held_act, held_slope, sems):
    def stores(lane, c):
        return (
            pltpu.make_async_copy(held_act.at[:, lane], activated.at[:, lane], sems.at[0, c]),
            pltpu.make_async_copy(held_slope.at[:, lane], slope.at[:, lane], sems.at[1, c]),
        )

    def step(lane, c):
        fill_extended(win, units, same, lane)
        for b in range(win.shape[0]):
            conv = convolve(win, b, taps, lane, False)
            q = jax.nn.sigmoid(conv)
            valid = valid_rows(fill, b)
            rows = slice(b * BLOCK, (b + 1) * BLOCK)
            held_act[rows, lane] = jnp.where(valid, conv * q, 0.0).astype(BF16)
            held_slope[rows, lane] = jnp.where(valid, q + conv * q * (1.0 - q), 0.0)
        for copy in stores(lane, c):
            copy.start()

    each_lane_block(units.shape[1], step)
    for c in range(units.shape[1] // LANES):
        for copy in stores(pl.ds(c * LANES, LANES), c):
            copy.wait()


def taps_kernel(same, units, grad_conv, out, win, sums):
    def step(lane, c):
        fill_extended(win, units, same, lane)
        sums[...] = jnp.zeros_like(sums)
        for b in range(win.shape[0]):
            grad = grad_conv[b * BLOCK : (b + 1) * BLOCK, lane]
            for shift in range(8):
                steps, rows = shifted(win, b, shift)
                for k, at in steps:
                    terms = (rows[at : at + BLOCK] * grad).reshape(BLOCK // 8, 8, LANES)
                    sums[k] += jnp.sum(terms, axis=0)
        out[:, lane] = jnp.sum(sums[...], axis=1)

    each_lane_block(units.shape[1], step)


def backward_kernel(same, fill, grad_conv, inner, outer, taps, value, gate, out, win):
    def step(lane, c):
        fill_windows(win, grad_conv, inner, outer, same, lane)
        for b in range(win.shape[0]):
            grad_units = jnp.where(valid_rows(fill, b), convolve(win, b, taps, lane, True), 0.0)
            rows = slice(b * BLOCK, (b + 1) * BLOCK)
            own = slice(b * BLOCK + HALO, (b + 1) * BLOCK + HALO)
            s = gate[own, lane]
            grad_value = grad_units * s
            out[0, rows, lane] = grad_value.astype(BF16)
            out[1, rows, lane] = (grad_value * value[own, lane] * (1.0 - s)).astype(BF16)

    each_lane_block(grad_conv.shape[1], step)


def norm_kernel(place, frames, inner, outer, gain, out, out_t):
    def rows(block):
        x = block.astype(F32)
        center = x - jnp.mean(x, axis=1, keepdims=True)
        inv = lax.rsqrt(jnp.mean(center * center, axis=1, keepdims=True) + EPSILON)
        return (center * inv * gain[...]).astype(BF16)

    for first in range(0, frames.shape[0], BLOCK):
        normed = rows(frames[first : first + BLOCK, :])
        out[HALO + first : HALO + first + BLOCK, :] = normed
        out_t[:, first : first + BLOCK] = normed.T
    odd = place[2] % 2 == 1
    out[:HALO, :] = rows(jnp.where(odd, inner[...].astype(F32), outer[...].astype(F32)))
    out[out.shape[0] - HALO :, :] = rows(jnp.where(odd, outer[...].astype(F32), inner[...].astype(F32)))


def chunks_kernel(section, rows, *refs):
    outs, held, sems = refs[:3], refs[3], refs[4]
    count = held.shape[2]
    loads, stores = [], []
    for i, out in enumerate(outs):
        first = pl.multiple_of((section[0] ^ (i + 1)) * count, count)
        loads.append(pltpu.make_async_copy(rows.at[:, pl.ds(first, count)], held.at[i], sems.at[0, i]))
        stores.append(pltpu.make_async_copy(held.at[i], out, sems.at[1, i]))
    for load in loads:
        load.start()
    for load, store in zip(loads, stores):
        load.wait()
        store.start()
    for store in stores:
        store.wait()


def gradient_kernel(section, own, first, second, third, weights, slope, arrived, out, sems):
    rows, count = first.shape
    here = pl.multiple_of(section[0] * count, count)
    pieces = own.at[:, pl.ds(here, count)], first, second, third
    copies = []
    for k, piece in enumerate(pieces):
        at = pl.multiple_of((section[0] ^ k) * rows, 64)
        copies.append(pltpu.make_async_copy(piece, arrived.at[pl.ds(at, rows), :], sems.at[k]))
    for copy in copies:
        copy.start()
    for copy in copies:
        copy.wait()
    grad = jnp.dot(weights[...], arrived[...], preferred_element_type=F32)
    out[...] = grad.T * slope[...]


def halves_kernel(core, rows, order, own, other, held, sem):
    copy = pltpu.make_async_copy(held, other, sem)
    for half, out in ((1 - core[0], held), (core[0], own)):
        for y in range(4):
            first = pl.multiple_of(y * 160 + half * 80, 16)
            second = pl.multiple_of((4 + y) * 160 + half * 80, 16)
            both = jnp.concatenate([rows[pl.ds(first, 80), :], rows[pl.ds(second, 80), :]], axis=0)
            moved = jnp.dot(order[...], both, preferred_element_type=F32)
            out[y * 160 : (y + 1) * 160, :] = moved.astype(BF16)
        if out is held:
            copy.start()
    copy.wait()


def final_kernel(sent, other, frames, arrived, gain, out):
    x = frames[...].astype(F32)
    center = x - jnp.mean(x, axis=1, keepdims=True)
    inv = lax.rsqrt(jnp.mean(center * center, axis=1, keepdims=True) + EPSILON)
    unit = center * inv
    e = (sent[...].astype(F32) + other[...].astype(F32)) * gain[...]
    back = e - jnp.mean(e, axis=1, keepdims=True) - unit * jnp.mean(e * unit, axis=1, keepdims=True)
    out[...] = (arrived[...].astype(F32).T + inv * back).astype(BF16)


def pair_kernel(first, left, left_peer, right, right_peer, *refs):
    out, held, sems = refs[-3:]
    groups, _, width = right.shape
    copies = []
    for g in range(groups):
        for at in range(0, width, 256):
            columns = slice(at, min(at + 256, width))
            total = jnp.dot(left[...], right[g, :, columns], preferred_element_type=F32)
            total = total + jnp.dot(left_peer[...], right_peer[g, :, columns], preferred_element_type=F32)
            made = pl.ds(g * width + at, columns.stop - at)
            held[:, made] = total.astype(BF16)
            there = pl.ds((first + g) * width + at, columns.stop - at)
            copies.append(pltpu.make_async_copy(held.at[:, made], out.at[:, there], sems.at[len(copies)]))
            copies[-1].start()
    for copy in copies:
        copy.wait()


def hbm():
    return pl.BlockSpec(memory_space=pltpu.HBM)


def smem():
    return pl.BlockSpec(memory_space=pltpu.SMEM)


def vmem():
    return pl.BlockSpec(memory_space=pltpu.VMEM)


def windows(count):
    return pltpu.VMEM((count // BLOCK, BLOCK + 2 * HALO, LANES), F32)


def convolved(same, fill, units, taps, count):
    width = units.shape[1]
    return pl.pallas_call(
        forward_kernel,
        in_specs=[smem(), smem(), vmem(), vmem()],
        out_specs=[hbm(), hbm()],
        out_shape=[pltpu.HBM((count, width), BF16), pltpu.HBM((count, width), F32)],
        scratch_shapes=[
            windows(count),
            pltpu.VMEM((count, width), BF16),
            pltpu.VMEM((count, width), F32),
            pltpu.SemaphoreType.DMA((2, width // LANES)),
        ],
        compiler_params=params(),
        cost_estimate=duration(5),
        name="conv_forward",
    )(same, fill, units, taps)


def tap_sums(same, units, grad_conv):
    count, width = grad_conv.shape
    return pl.pallas_call(
        taps_kernel,
        in_specs=[smem(), vmem(), vmem()],
        out_specs=vmem(),
        out_shape=jax.ShapeDtypeStruct((32, width), F32),
        scratch_shapes=[windows(count), pltpu.VMEM((32, 8, LANES), F32)],
        compiler_params=params(),
        cost_estimate=duration(4),
        name="tap_gradients",
    )(same, units, grad_conv)


def projected_back(same, fill, grad_conv, inner, outer, taps, value, gate):
    count, width = grad_conv.shape
    return pl.pallas_call(
        backward_kernel,
        in_specs=[smem(), smem()] + [vmem()] * 6,
        out_specs=vmem(),
        out_shape=jax.ShapeDtypeStruct((2, count, width), BF16),
        scratch_shapes=[windows(count)],
        compiler_params=params(),
        cost_estimate=duration(5.6),
        name="conv_backward",
    )(same, fill, grad_conv, inner, outer, taps, value, gate)


def normalised(place, frames, inner, outer, gain):
    count, features = frames.shape
    return pl.pallas_call(
        norm_kernel,
        in_specs=[smem()] + [vmem()] * 4,
        out_specs=[vmem(), vmem()],
        out_shape=[
            jax.ShapeDtypeStruct((count + 2 * HALO, features), BF16),
            jax.ShapeDtypeStruct((features, count), BF16),
        ],
        compiler_params=params(),
        cost_estimate=duration(3.5),
        name="layer_norm",
    )(place, frames, inner, outer, gain.reshape(1, features))


def frame_chunks(section, rows):
    features, total = rows.shape
    count = total // 4
    return pl.pallas_call(
        chunks_kernel,
        in_specs=[smem(), hbm()],
        out_specs=[hbm()] * 3,
        out_shape=[pltpu.HBM((features, count), rows.dtype)] * 3,
        scratch_shapes=[pltpu.VMEM((3, features, count), rows.dtype), pltpu.SemaphoreType.DMA((2, 3))],
        compiler_params=params(),
        cost_estimate=duration(2),
        name="frame_chunks",
    )(section, in_hbm(rows))


def conv_gradient(section, pieces, weights, slope):
    features, count = 4 * pieces[1].shape[0], pieces[1].shape[1]
    return pl.pallas_call(
        gradient_kernel,
        in_specs=[smem()] + [hbm()] * 4 + [vmem()] * 2,
        out_specs=[vmem()] * 2,
        out_shape=[
            jax.ShapeDtypeStruct((features, count), BF16),
            jax.ShapeDtypeStruct((count, weights.shape[0]), F32),
        ],
        scratch_shapes=[pltpu.SemaphoreType.DMA((4,))],
        compiler_params=params(),
        cost_estimate=duration(3),
        name="conv_gradient",
    )(section, *[in_hbm(piece) for piece in pieces], weights, slope)


def halves(core, rows, keep=False):
    features, count = rows.shape
    order = np.zeros((160, 160), np.float32)
    for z in range(4):
        for x in range(2):
            for r in range(20):
                order[(z * 2 + x) * 20 + r, x * 80 + z * 20 + r] = 1.0
    half = jax.ShapeDtypeStruct((features // 2, count), BF16)
    return pl.pallas_call(
        halves_kernel,
        in_specs=[smem(), vmem(), vmem()],
        out_specs=[vmem(), hbm()],
        out_shape=[half if keep else pltpu.HBM(half.shape, BF16), pltpu.HBM(half.shape, BF16)],
        scratch_shapes=[pltpu.VMEM(half.shape, BF16), pltpu.SemaphoreType.DMA],
        compiler_params=params(),
        cost_estimate=duration(1.2),
        name="core_halves",
    )(core.reshape(1), rows, jnp.asarray(order, BF16))


def norm_back(sent, other, frames, arrived, gain):
    count, features = frames.shape
    block = pl.BlockSpec((BLOCK, features), lambda i: (i, 0))
    return pl.pallas_call(
        final_kernel,
        grid=(count // BLOCK,),
        in_specs=[
            block,
            block,
            block,
            pl.BlockSpec((features, BLOCK), lambda i: (0, i)),
            pl.BlockSpec((1, features), lambda i: (0, 0)),
        ],
        out_specs=block,
        out_shape=jax.ShapeDtypeStruct((count, features), BF16),
        compiler_params=params(),
        cost_estimate=duration(10.4),
        name="norm_backward",
    )(in_hbm(sent), in_hbm(other), in_hbm(frames), in_hbm(arrived), gain)


def pair_product(left, left_peer, right, right_peer, groups, first, buffer=None):
    rows = left.shape[0]
    made, _, width = right.shape
    return pl.pallas_call(
        functools.partial(pair_kernel, first),
        in_specs=[vmem()] * 4 + ([] if buffer is None else [hbm()]),
        out_specs=hbm(),
        out_shape=pltpu.HBM((rows, groups * width), BF16),
        scratch_shapes=[pltpu.VMEM((rows, made * width), BF16), pltpu.SemaphoreType.DMA((3 * made,))],
        input_output_aliases={} if buffer is None else {4: 0},
        compiler_params=params(),
        cost_estimate=duration(3.4),
        name="weight_gradient",
    )(left, left_peer, right, right_peer, *([] if buffer is None else [in_hbm(buffer)]))


def shares_of(value, axis):
    return [value] + [lax.ppermute(value, axis, [(i, i ^ k) for i in range(4)]) for k in (1, 2, 3)]


def sum_of(shares):
    own, first, second, third = [share.astype(F32) for share in shares]
    return (own + first) + (second + third)


def finish_rows(summed, xl):
    own = lax.dynamic_index_in_dim(summed, xl, 0, keepdims=False)
    other = lax.dynamic_index_in_dim(summed, 1 - xl, 0, keepdims=False)
    return own + swap(other.astype(BF16), "xl").astype(F32)


def body(frames, returned, norm_gain, weight_in, kernel, weight_out, block_utt, block_fill):
    count = frames.shape[0]
    width = weight_in.shape[2]
    features = frames.shape[1]
    blocks = count // BLOCK
    core, xl = lax.axis_index("core"), lax.axis_index("xl")
    first_block = lax.axis_index(FRAMES) * blocks
    place = jnp.stack([core, lax.axis_index("y"), lax.axis_index("section")]).astype(jnp.int32)
    section = lax.axis_index("section").reshape(1)
    *chunks, frames = lax.optimization_barrier((*frame_chunks(section, returned.T), frames))
    pieces = [returned.T]
    for k, chunk in enumerate(chunks, 1):
        pieces.append(lax.ppermute(chunk, "section", [(i, i ^ k) for i in range(4)]))

    edge = jnp.full((1,), -1, jnp.int32)
    near_utt = lax.dynamic_slice(jnp.concatenate([edge, block_utt, edge]), (first_block,), (blocks + 2,))
    near_fill = lax.dynamic_slice(jnp.concatenate([edge, block_fill, edge]), (first_block,), (blocks + 2,))
    same = (near_utt[1:] == near_utt[:-1]).astype(jnp.int32)
    same = jnp.concatenate([same, lax.axis_index(FRAMES)[None].astype(jnp.int32) % 2])
    fill = near_fill[1:-1]
    valid = (jnp.arange(BLOCK, dtype=jnp.int32)[None, :] < near_fill[:, None]).reshape(-1)
    valid = valid[BLOCK - HALO : BLOCK + count + HALO]

    normed_ext, normed_t = normalised(place, frames, *halos(frames), norm_gain)
    value_proj = jnp.dot(normed_ext, weight_in[0], preferred_element_type=F32)
    gate_proj = jnp.dot(normed_ext, weight_in[1], preferred_element_type=F32)
    gate_sigmoid = jax.nn.sigmoid(gate_proj)
    units = jnp.where(valid[:, None], value_proj * gate_sigmoid, 0.0).astype(BF16)
    activated, slope = convolved(same, fill, units, kernel, count)
    activated_peer = swap(activated, "core")

    normed_own, normed_other = halves(core, normed_t)
    normed_peer = swap(normed_other, "core")

    arrived, grad_conv = conv_gradient(section, pieces, weight_out, slope)
    normed_own, normed_other, grad_conv = lax.optimization_barrier((normed_own, normed_other, grad_conv))
    conv_inner, conv_outer = halos(grad_conv.astype(BF16))
    arrived_rows, grad_conv = lax.optimization_barrier((arrived, grad_conv))
    rows_own, rows_other = halves(core, arrived_rows, keep=True)
    rows_peer = swap(rows_other, "core")
    parts = pair_product(rows_own, rows_peer, activated[None], activated_peer[None], 3, 0)

    ready, parts = lax.optimization_barrier((grad_conv, parts))
    late = projected_back(
        same, fill, ready, conv_inner, conv_outer, kernel, value_proj, gate_sigmoid
    )
    late_peer = swap(late, "core")
    contract = (((0, 2), (0, 2)), ((), ()))
    sent = lax.dot_general(late, weight_in, contract, preferred_element_type=F32).astype(BF16)
    other = swap(sent, "tensor")
    late, sent = lax.optimization_barrier((late, sent))
    parts = pair_product(normed_own, normed_peer, late, late_peer, 3, 1, parts)
    got = lax.all_to_all(parts.reshape(16, 40, 3 * width), PLANE, 0, 0)

    ready, sent_again, _ = lax.optimization_barrier((grad_conv, sent, parts))
    taps_part = tap_sums(same, units, ready)
    gain_part = sent_again.astype(F32) * normed_ext[HALO : HALO + count].astype(F32)
    gain_part = jnp.sum(gain_part, axis=0) / norm_gain
    small = jnp.concatenate([taps_part, gain_part.reshape(2, width)], axis=0)
    small = small + swap(small, "core")
    gain = small[32:]
    corner = lax.ppermute(gain, ("xl", "tensor"), [(0, 3), (1, 2), (2, 1), (3, 0)])
    across = swap(small, "xl"), swap(gain, "tensor"), corner
    grad_frames = norm_back(sent, other, frames, arrived, norm_gain.reshape(1, features))
    small, across, grad_frames = lax.optimization_barrier((small, across, grad_frames))
    gain = (small[32:] + across[1]) + (across[0][32:] + across[2])
    small = jnp.concatenate([small[:32] + across[0][:32], gain], axis=0)
    shares = shares_of(small.astype(BF16), "y")
    got, grad_frames = lax.optimization_barrier((got, grad_frames))
    total = jnp.sum(got.astype(F32), axis=0)
    total, shares = lax.optimization_barrier((total, shares))
    summed = finish_rows(total.reshape(2, 20, 3 * width), xl)
    grad_out = summed[:, :width].T
    grad_in = summed[:, width:].reshape(20, 2, width).transpose(1, 0, 2)
    shares = shares_of(sum_of(shares).astype(BF16), "section")
    grad_in, grad_out, shares = lax.optimization_barrier((grad_in, grad_out, shares))
    small = sum_of(shares)
    grad_kernel = small[:TAPS]
    grad_gain = small[32:].reshape(features)
    return (grad_frames, grad_in, grad_out, grad_kernel, grad_gain)


def solution(mesh):
    split = Mesh(
        np.asarray(mesh.devices).reshape(2, 4, 2, 2, 4), ("xl", "y", "core", "tensor", "section")
    )
    outer = ("xl", "y", "core")
    in_specs = (
        P(FRAMES, None),
        P(outer, "section"),
        P(),
        P(None, None, "tensor"),
        P(None, "tensor"),
        P("tensor", None),
        P(),
        P(),
    )
    out_specs = (
        P(FRAMES, None),
        P(None, FRAMES, "tensor"),
        P("tensor", FRAMES),
        P(None, "tensor"),
        P(),
    )
    return jax.shard_map(body, mesh=split, in_specs=in_specs, out_specs=out_specs, check_vma=False)
```
